32 devices in a mesh: seq: 8 (over y, x, core), head: 4 (over z).
Axes of the slice: x: 2, y: 2, z: 4, core: 2. Of those that a mesh axis runs over, the one named last changes fastest.
Arguments:
- residual_in: bfloat16 [4, 4096, 1536], P(None, 'seq'), may hold values from -6 to 6
- lengths: int32 [4], replicated, may hold values from 1024 to 4096, as said below
- norm_gain: float32 [1536], replicated, may hold values from 0.5 to 1.5
- gate_projection_weight: bfloat16 [1536, 3072], P(None, 'head'), may hold values from -0.15625 to 0.15625
- head_channels_weight: bfloat16 [1536, 3072], P(None, 'head'), may hold values from -0.15625 to 0.15625
- input_state_pair_weight: bfloat16 [1536, 256], P(None, 'head'), may hold values from -0.15625 to 0.15625
- step_size_weight: bfloat16 [1536, 48], P(None, 'head'), may hold values from -0.15625 to 0.15625
- x_taps: float32 [4, 3072], P(None, 'head'), may hold values from -2.5 to 2.5
- bc_taps: float32 [4, 256], P(None, 'head'), may hold values from -2.5 to 2.5
- x_bias: float32 [3072], P('head'), may hold values from -1.5 to 1.5
- bc_bias: float32 [256], P('head'), may hold values from -1.5 to 1.5
- step_bias: float32 [48], P('head'), may hold values from -4 to -2
- decay_log: float32 [48], P('head'), may hold values from -6 to -1
- skip_gain: float32 [48], P('head'), may hold values from 0.5 to 1.5
- out_gain: float32 [3072], P('head'), may hold values from 0.5 to 1.5
- output_projection_weight: bfloat16 [3072, 1536], P('head'), may hold values from -0.109375 to 0.109375
- cotangent: bfloat16 [4, 4096, 1536], P(None, 'seq'), may hold values from -6 to 6
Outputs:
- result: bfloat16 [4, 4096, 1536], P(None, 'seq')
- grad_input: float32 [4, 4096, 1536], P(None, 'seq')
- grad_norm_gain: float32 [1536], replicated
- grad_z_weight: float32 [1536, 3072], P(None, 'head')
- grad_x_weight: float32 [1536, 3072], P(None, 'head')
- grad_bc_weight: float32 [1536, 256], P(None, 'head')
- grad_step_weight: float32 [1536, 48], P(None, 'head')
- grad_x_taps: float32 [4, 3072], P(None, 'head')
- grad_bc_taps: float32 [4, 256], P(None, 'head')
- grad_x_bias: float32 [3072], P('head')
- grad_bc_bias: float32 [256], P('head')
- grad_step_bias: float32 [48], P('head')
- grad_decay_log: float32 [48], P('head')
- grad_skip_gain: float32 [48], P('head')
- grad_out_gain: float32 [3072], P('head')
- grad_out_weight: float32 [3072, 1536], P('head')
The draws below stay inside these ranges and needn't reach their ends.
Inputs may be any that keep to these rules, and one draw needn't show every extreme that they name: `lengths`: one sequence, drawn from the seed, has all 4096 slots valid and another has 1024; the valid slots of a sequence are its first ones.
All inputs are finite; a program needn't handle non-finite values.
Results may differ from the reference program's by a relative error of at most 0.00145.
The reference program's roundings to bfloat16 on the way count: a program that leaves them out, or rounds other values in their place, can miss the bound.
Values may be sent and summed in bfloat16 or wider, within the bound.
No kernel may reach another device: no remote copies, remote signals or barrier semaphores. Data moves between devices by JAX's collectives and lax.ppermute only.
A program may use at most 448 MiB of HBM per device.

```python
import math
from functools import partial
import jax
import jax.numpy as jnp
from jax import lax

D = 1536
HEADS = 48
HEAD_DIM = 64
STATE = 128
CONV = 4
GROUP = 256
INNER = 3072
SEQS = 4
SLOTS = 4096


def draw_lengths(key, part):
    key = jax.random.fold_in(key, 3)
    first_key, second_key = jax.random.split(key)
    drawn = jax.random.randint(first_key, (SEQS,), SLOTS // 4, SLOTS + 1)
    ranking = jax.random.permutation(second_key, SEQS)
    drawn = drawn.at[ranking[0]].set(SLOTS)
    return drawn.at[ranking[1]].set(SLOTS // 4).astype(jnp.int32)


def draw_decay_log(key, part):
    key = jax.random.fold_in(key, 7)
    lowest = max(min(math.log(1.0 / (0.03 * SLOTS)), -2.0), -6.0)
    return jax.random.uniform(key, (HEADS,), jnp.float32, lowest, -1.0)


def levels(rng, shape, cuts, least, largest):
    factor_of = 1.0
    for dim, blocks in cuts:
        draws = jax.random.uniform(jax.random.fold_in(jax.random.fold_in(rng, 6), dim), (blocks,), jnp.float32, least / len(cuts), largest / len(cuts))
        factor_of = factor_of * jnp.repeat(jnp.exp(draws), shape[dim] // blocks).reshape((-1,) + (1,) * (len(shape) - 1 - dim))
    return factor_of


def normal_values(own_key, dims, width, bound, cuts=(), dtype=jnp.bfloat16):
    factor_of = levels(own_key, dims, cuts, -0.22, 0.18) if cuts else 1.0
    values = jax.random.normal(own_key, dims, jnp.float32) * width * factor_of
    return jnp.minimum(jnp.maximum(values, -bound), bound).astype(dtype)


def setup_inputs(seed: int = 0) -> dict:
    key_of = jax.random.split(jax.random.key(seed), 18)
    return {
        "residual_in": normal_values(key_of[0], (SEQS, SLOTS, D), 1.0, 6.0, ((1, 8),)),
        "lengths": draw_lengths(jax.random.fold_in(key_of[17], 71), 0),
        "norm_gain": jnp.clip(1.0 + 0.1 * jax.random.normal(key_of[2], (D,), jnp.float32), 0.5, 1.5),
        "gate_projection_weight": normal_values(key_of[3], (D, INNER), D ** -0.5, 0.15625, ((1, 4),)),
        "head_channels_weight": normal_values(key_of[4], (D, INNER), D ** -0.5, 0.15625, ((1, 4),)),
        "input_state_pair_weight": normal_values(key_of[5], (D, 2 * STATE), D ** -0.5, 0.15625, ((1, 4),)),
        "step_size_weight": normal_values(key_of[6], (D, HEADS), D ** -0.5, 0.15625, ((1, 4),)),
        "x_taps": normal_values(key_of[7], (CONV, INNER), 0.5, 2.5, ((1, 4),), jnp.float32),
        "bc_taps": normal_values(key_of[8], (CONV, 2 * STATE), 0.5, 2.5, ((1, 4),), jnp.float32),
        "x_bias": normal_values(key_of[9], (INNER,), 0.3, 1.5, ((0, 4),), jnp.float32),
        "bc_bias": normal_values(key_of[10], (2 * STATE,), 0.3, 1.5, ((0, 4),), jnp.float32),
        "step_bias": jnp.clip(-4.0 + 2.0 * jax.random.uniform(key_of[11], (HEADS,), jnp.float32) ** levels(key_of[11], (HEADS,), ((0, 4),), -0.2, 0.2), -4.0, -2.0),
        "decay_log": draw_decay_log(jax.random.fold_in(key_of[17], 71), 0),
        "skip_gain": jnp.clip(0.5 + 1.0 * jax.random.uniform(key_of[13], (HEADS,), jnp.float32) ** levels(key_of[13], (HEADS,), ((0, 4),), -0.2, 0.2), 0.5, 1.5),
        "out_gain": jnp.clip(1.0 + 0.1 * jax.random.normal(key_of[14], (INNER,), jnp.float32), 0.5, 1.5),
        "output_projection_weight": normal_values(key_of[15], (INNER, D), INNER ** -0.5, 0.109375, ((0, 4),)),
        "cotangent": normal_values(key_of[16], (SEQS, SLOTS, D), 1.0, 6.0, ((1, 8),)),
    }


EPSILON = 1e-05
MATMUL_ACCURACY = lax.Precision.HIGHEST

@jax.custom_vjp
def low(v):
    return lax.optimization_barrier(v.astype(jnp.bfloat16)).astype(jnp.float32)

@jax.custom_vjp
def reduced_precision_backward(v):
    return v

def low_keep(v):
    return (low(v), None)

def low_pass(kept, grad):
    return (grad,)

def back_keep(v):
    return (v, None)

def back_low(kept, grad):
    return (low(grad),)
low.defvjp(low_keep, low_pass)
reduced_precision_backward.defvjp(back_keep, back_low)

def convolve(extended, taps, offset_bias, length):
    summed = offset_bias + taps[0] * extended[:, 0:length]
    for tap_index in range(1, taps.shape[0]):
        summed = summed + taps[tap_index] * extended[:, tap_index:tap_index + length]
    return summed

def block_math(block_x, block_b, block_c, block_step, block_rate, state_in):
    cumulative = jnp.cumsum(block_rate, axis=-1)
    length = block_rate.shape[-1]
    lower_mask = lax.iota(jnp.int32, length)[:, None] >= lax.iota(jnp.int32, length)[None, :]
    gap_matrix = cumulative[..., :, None] - cumulative[..., None, :]
    kernel = jnp.where(lower_mask, jnp.exp(jnp.where(lower_mask, gap_matrix, 0.0)), 0.0)
    intersection_scores = jnp.einsum('sln,smn->slm', block_c, block_b, precision=MATMUL_ACCURACY)
    mixing = kernel * intersection_scores[:, None] * block_step[..., None, :]
    carried = jnp.einsum('sln,shpn->shlp', block_c, state_in, precision=MATMUL_ACCURACY)
    output = jnp.einsum('shlm,shmp->shlp', mixing, block_x, precision=MATMUL_ACCURACY) + jnp.exp(cumulative)[..., None] * carried
    ending = cumulative[..., -1:]
    weighted = (jnp.exp(ending - cumulative) * block_step)[..., None] * block_x
    updated = jnp.exp(ending)[..., None] * state_in + jnp.einsum('shlp,sln->shpn', weighted, block_b, precision=MATMUL_ACCURACY)
    return (output, updated, cumulative)

def scan_sequence(heads_view, b_all, c_all, step, rate):
    seq_count = heads_view.shape[0]
    blocks = heads_view.shape[1] // GROUP
    xs_blocks = heads_view.reshape(seq_count, blocks, GROUP, HEADS, HEAD_DIM).transpose(1, 0, 3, 2, 4)
    b_blocks = b_all.reshape(seq_count, blocks, GROUP, STATE).transpose(1, 0, 2, 3)
    c_blocks = c_all.reshape(seq_count, blocks, GROUP, STATE).transpose(1, 0, 2, 3)
    step_blocks = step.reshape(seq_count, blocks, GROUP, HEADS).transpose(1, 0, 3, 2)
    rate_blocks = rate.reshape(seq_count, blocks, GROUP, HEADS).transpose(1, 0, 3, 2)

    def advance(state_in, pieces):
        output, updated, cumulative = block_math(pieces[0], pieces[1], pieces[2], pieces[3], pieces[4], state_in)
        return (updated, output)
    start_state = jnp.zeros((seq_count, HEADS, HEAD_DIM, STATE), jnp.float32)
    final_state, outputs = lax.scan(jax.checkpoint(advance), start_state, (xs_blocks, b_blocks, c_blocks, step_blocks, rate_blocks))
    return outputs.transpose(1, 0, 3, 2, 4).reshape(seq_count, blocks * GROUP, HEADS * HEAD_DIM)

def forward(valid_mask, inputs, norm_gain, gate_projection_weight, head_channels_weight, input_state_pair_weight, step_size_weight, x_taps, bc_taps, x_bias, bc_bias, step_bias, decay_log, skip_gain, out_gain, output_projection_weight):
    scale_in = lax.rsqrt(lax.optimization_barrier(jnp.mean(inputs * inputs, axis=-1, keepdims=True)) + EPSILON)
    normalized_rows = low(inputs * scale_in * norm_gain)
    gate_before_activation = reduced_precision_backward(jnp.einsum('aym,mq->ayq', normalized_rows, gate_projection_weight, precision=MATMUL_ACCURACY))
    head_channels_raw = reduced_precision_backward(jnp.einsum('aym,mq->ayq', normalized_rows, head_channels_weight, precision=MATMUL_ACCURACY))
    input_state_pair_raw = reduced_precision_backward(jnp.einsum('aym,mq->ayq', normalized_rows, input_state_pair_weight, precision=MATMUL_ACCURACY))
    step_size_raw = reduced_precision_backward(jnp.einsum('aym,mq->ayq', normalized_rows, step_size_weight, precision=MATMUL_ACCURACY))
    padding = ((0, 0), (CONV - 1, 0), (0, 0))
    xs = jax.nn.silu(convolve(jnp.pad(head_channels_raw, padding), x_taps, x_bias, SLOTS))
    bc_all = jax.nn.silu(convolve(jnp.pad(input_state_pair_raw, padding), bc_taps, bc_bias, SLOTS))
    step = jax.nn.softplus(step_size_raw + step_bias)
    rate = -step * jnp.exp(decay_log)
    seq_count = inputs.shape[0]
    heads_view = xs.reshape(seq_count, SLOTS, HEADS, HEAD_DIM)
    mixed = scan_sequence(heads_view, bc_all[..., :STATE], bc_all[..., STATE:], step, rate)
    mixed = mixed + (heads_view * skip_gain[:, None]).reshape(seq_count, SLOTS, HEADS * HEAD_DIM)
    gated = mixed * jax.nn.silu(gate_before_activation)
    gate_scale = lax.rsqrt(lax.optimization_barrier(jnp.mean(gated * gated, axis=-1, keepdims=True)) + EPSILON)
    hidden_rows = low(gated * gate_scale * out_gain)
    residual_branch = jnp.einsum('kmq,qh->kmh', hidden_rows, output_projection_weight, precision=MATMUL_ACCURACY)
    return (inputs + residual_branch) * valid_mask[..., None]

def reference(residual_in, lengths, norm_gain, gate_projection_weight, head_channels_weight, input_state_pair_weight, step_size_weight, x_taps, bc_taps, x_bias, bc_bias, step_bias, decay_log, skip_gain, out_gain, output_projection_weight, cotangent):
    valid_mask = (lax.iota(jnp.int32, SLOTS)[None, :] < lengths[:, None]).astype(jnp.float32)
    floats = (residual_in.astype(jnp.float32), norm_gain.astype(jnp.float32), gate_projection_weight.astype(jnp.float32), head_channels_weight.astype(jnp.float32), input_state_pair_weight.astype(jnp.float32), step_size_weight.astype(jnp.float32), x_taps.astype(jnp.float32), bc_taps.astype(jnp.float32), x_bias.astype(jnp.float32), bc_bias.astype(jnp.float32), step_bias.astype(jnp.float32), decay_log.astype(jnp.float32), skip_gain.astype(jnp.float32), out_gain.astype(jnp.float32), output_projection_weight.astype(jnp.float32))
    output, backward = jax.vjp(partial(forward, valid_mask), *floats)
    grads = backward(cotangent.astype(jnp.float32))
    return (output.astype(jnp.bfloat16), grads[0], grads[1], grads[2], grads[3], grads[4], grads[5], grads[6], grads[7], grads[8], grads[9], grads[10], grads[11], grads[12], grads[13], grads[14])
```

```python
import functools

import jax
import jax.numpy as jnp
from jax import lax
from jax.experimental import pallas as pl
from jax.experimental.pallas import tpu as pltpu
from jax.sharding import PartitionSpec as P

HEAD_DIM = 64
STATE = 128
CONV = 4
INNER = 3072
CHUNK = 128
ROWS = 256
HALF = 64
LANES = 128
EPSILON = 1e-05
GROUPS = 2
F32 = jnp.float32
BF16 = jnp.bfloat16
F16 = jnp.float16
I32 = jnp.int32
VMEM_LIMIT = 60 * 1024 * 1024


def halves(value):
    high = value.astype(BF16)
    return high, (value - high.astype(F32)).astype(BF16)


def thirds(value):
    high = value.astype(BF16)
    rest = value - high.astype(F32)
    middle = rest.astype(BF16)
    return high, middle, (rest - middle.astype(F32)).astype(BF16)


def mm(a, b, ca=1, cb=0):
    return lax.dot_general(a, b, (((ca,), (cb,)), ((), ())), preferred_element_type=F32)


def dot3(a, b):
    return mm(jnp.concatenate([a[0], a[1]], axis=1), jnp.concatenate([b[0], b[0]], axis=0)) + mm(a[0], b[1])


def dot3_t(a, b):
    n = b[0].shape[0]
    wide = mm(a[0], jnp.concatenate([b[0], b[1]], axis=0), 1, 1)
    return wide[:, :n] + wide[:, n:] + mm(a[1], b[0], 1, 1)


def per_head(value, expand):
    high, low = halves(value)
    return mm(high, expand, 1, 1) + mm(low, expand, 1, 1)


def summed_by(matrix, value):
    out = None
    for part in thirds(value):
        term = mm(matrix, part)
        out = term if out is None else out + term
    return out


def rows8(row):
    return jnp.broadcast_to(row, (8, row.shape[-1]))


def fold8(value):
    return jnp.sum(value.reshape(value.shape[0] // 8, 8, value.shape[1]), axis=0)


def peak8(value):
    return jnp.max(jnp.abs(value).reshape(value.shape[0] // 8, 8, value.shape[1]), axis=0)


def left_half(rows):
    return lax.broadcasted_iota(jnp.int32, (rows, LANES), 1) < HEAD_DIM


def spread_pair(value, pair, left):
    h = 2 * pair
    return jnp.where(left, value[:, h : h + 1], value[:, h + 1 : h + 2])


def spread(value, channels):
    left = left_half(value.shape[0])
    return jnp.concatenate([spread_pair(value, j, left) for j in range(channels // LANES)], axis=1)


def softplus(value):
    small = jnp.exp(-jnp.abs(value))
    one = 1.0 + small
    log = jnp.where(one == 1.0, small, jnp.log(one) * (small / jnp.where(one == 1.0, 1.0, one - 1.0)))
    return jnp.maximum(value, 0.0) + log


def sigmoid(value):
    return 1.0 / (1.0 + jnp.exp(-value))


def conv(ext_ref, taps_ref, bias_ref, start, length, lanes):
    summed = bias_ref[0:1, lanes] + taps_ref[0:1, lanes] * ext_ref[start + 5 : start + 5 + length, lanes]
    for k in range(1, CONV):
        summed = summed + taps_ref[k : k + 1, lanes] * ext_ref[start + 5 + k : start + 5 + k + length, lanes]
    return summed


def conv_back(grad_ref, taps_ref, start, length, lanes):
    raw = taps_ref[CONV - 1 : CONV, lanes] * grad_ref[start : start + length, lanes]
    for j in range(1, CONV):
        raw = raw + taps_ref[CONV - 1 - j : CONV - j, lanes] * grad_ref[start + j : start + j + length, lanes]
    return raw


def as_column(row):
    return jnp.broadcast_to(row, (LANES, LANES)).T


def row_sums(value):
    ones = jnp.ones((8, LANES), BF16)
    parts = thirds(value)
    return mm(ones, parts[0], 1, 1) + (mm(ones, parts[1], 1, 1) + mm(ones, parts[2], 1, 1))


def triangle(length, lower):
    row = lax.broadcasted_iota(jnp.int32, (length, length), 0)
    column = lax.broadcasted_iota(jnp.int32, (length, length), 1)
    return row >= column if lower else row <= column


ANYWHERE = pl.BlockSpec(memory_space=pl.ANY)


class Order:
    def __init__(self):
        self.now, self.pending, self.used = None, [], 0

    def before_next(self, *arrays):
        self.pending += [array for array in arrays if array.dtype != F16]

    def fence(self):
        tokens = self.pending + ([] if self.now is None else [self.now])
        self.pending = []

        def body(*refs):
            refs[-1][...] = jnp.zeros_like(refs[-1])

        self.now = pl.pallas_call(
            body,
            in_specs=[ANYWHERE] * len(tokens),
            out_shape=SHAPE((8, LANES), F32),
            compiler_params=pltpu.CompilerParams(vmem_limit_bytes=VMEM_LIMIT),
            name="fence",
        )(*tokens)

    def tie(self, value):
        if self.now is None:
            return value
        self.used += 1
        at = (self.used // LANES % 8, self.used % LANES)
        return value + lax.slice(self.now, at, (at[0] + 1, at[1] + 1)).reshape(()).astype(value.dtype)

    def call(self, kernel, operands, *, meta, grid, in_specs, out_specs, out_shape, scratch=(), flops, moved, name, aliases=None):
        tokens = self.pending + ([] if self.now is None else [self.now])
        inputs, outputs = len(operands), len(out_shape)
        self.pending = []

        def body(meta_ref, *refs):
            last = inputs + len(tokens) + outputs
            refs[last][...] = jnp.zeros_like(refs[last])
            kernel(meta_ref, *refs[:inputs], *refs[inputs + len(tokens) : last], *refs[last + 1 :])

        result = pl.pallas_call(
            body,
            grid_spec=pltpu.PrefetchScalarGridSpec(
                num_scalar_prefetch=1,
                grid=grid,
                in_specs=list(in_specs) + [ANYWHERE] * len(tokens),
                out_specs=list(out_specs) + [whole((8, LANES))],
                scratch_shapes=list(scratch),
            ),
            out_shape=list(out_shape) + [SHAPE((8, LANES), F32)],
            input_output_aliases=aliases or {},
            compiler_params=pltpu.CompilerParams(
                vmem_limit_bytes=VMEM_LIMIT, dimension_semantics=("arbitrary",) * len(grid)
            ),
            cost_estimate=pl.CostEstimate(flops=int(flops), bytes_accessed=int(moved), transcendentals=0),
            name=name,
        )(meta, *operands, *tokens)
        self.now = result[-1]
        return result[:-1]


def constants_kernel(lengths_ref, step_bias_ref, decay_ref, skip_ref, out_gain_ref, meta_ref, head_ref, chan_ref, expand_ref, *, slots):
    seqs, heads = lengths_ref.shape[0], step_bias_ref.shape[1]
    channels = out_gain_ref.shape[1]
    place, least = jnp.int32(0), lengths_ref[0]
    for s in range(1, seqs):
        shorter = lengths_ref[s] < least
        place, least = jnp.where(shorter, s, place), jnp.where(shorter, lengths_ref[s], least)
    first = lax.axis_index("seq") * slots
    for s in range(seqs):
        source = jnp.where(place == s, seqs - 1, s) if s < seqs - 1 else place
        meta_ref[s] = source
        meta_ref[seqs + s] = lengths_ref[source] - first
    mine, count = lax.axis_index("head"), lax.axis_size("head")
    meta_ref[2 * seqs] = jnp.where((mine == 0) | (mine == count - 1), 1, 0)
    lane = lax.broadcasted_iota(jnp.int32, (8, LANES), 1)
    row = lax.broadcasted_iota(jnp.int32, (8, LANES), 0)
    pad = lambda ref: jnp.concatenate([ref[...], jnp.zeros((1, LANES - heads), F32)], axis=1)
    head_ref[...] = jnp.zeros((8, LANES), F32)
    head_ref[0:1, :] = pad(step_bias_ref)
    head_ref[1:2, :] = pad(decay_ref)
    chan_ref[...] = jnp.zeros_like(chan_ref)
    chan_ref[0:1, :] = spread(rows8(pad(skip_ref)), channels)[0:1, :]
    chan_ref[1:2, :] = out_gain_ref[...]
    head_of = lax.broadcasted_iota(jnp.int32, (LANES, channels), 1) // HEAD_DIM
    expand_ref[...] = jnp.where(head_of == lax.broadcasted_iota(jnp.int32, (LANES, channels), 0), 1.0, 0.0).astype(BF16)


def normalized(rows, gain):
    u = rows.astype(F32)
    scale = lax.rsqrt(jnp.mean(u * u, axis=-1, keepdims=True) + EPSILON)
    return (u * scale * gain).astype(BF16)


def project_kernel(
    meta_ref, u_ref, cot_ref, gain_ref, gate_ref, x_ref, step_ref, out_ref, normed_ref, branch_ref, proj_ref, gh_ref, *, first
):
    rows, channels = u_ref.shape[0], gate_ref.shape[1]
    normed = normalized(u_ref[...], gain_ref[...])
    normed_ref[...] = normed
    at = pl.program_id(1) * rows + lax.broadcasted_iota(jnp.int32, cot_ref.shape, 0)
    live = at < meta_ref[4 + first + pl.program_id(0)]
    branch = jnp.where(live, cot_ref[...].astype(F32), 0.0).astype(BF16)
    branch_ref[...] = branch
    proj_ref[:, :channels] = mm(normed, gate_ref[...])
    proj_ref[:, channels : 2 * channels] = mm(normed, x_ref[...])
    proj_ref[:, 2 * channels :] = mm(normed, step_ref[...])
    gh_ref[...] = mm(branch, out_ref[...])


def edge_kernel(meta_ref, before_ref, gain_ref, x_ref, pair_ref, xhalo_ref, bchalo_ref):
    seqs, rows, width = before_ref.shape
    normed = normalized(before_ref[...].reshape(seqs * rows, width), gain_ref[...])
    xhalo_ref[...] = mm(normed, x_ref[...]).reshape(xhalo_ref.shape)
    bchalo_ref[...] = mm(normed, pair_ref[...]).reshape(bchalo_ref.shape)


def local_state_kernel(
    meta_ref, x_ref, xhalo_ref, normed_ref, pair_ref, bchalo_ref, step_ref, taps_ref, bias_ref, btaps_ref, bbias_ref,
    head_ref, xs_ref, raw_ref, bcs_ref, sc_ref, end_ref, xe, be, state, total,
):
    c, rows = pl.program_id(1), x_ref.shape[0]
    channels = x_ref.shape[1]

    @pl.when(c == 0)
    def _():
        xe[0:8, :] = xhalo_ref[...]
        be[0:8, :] = bchalo_ref[...]
        state[...] = jnp.zeros_like(state)
        total[...] = jnp.zeros_like(total)

    xe[8 : 8 + rows, :] = x_ref[...]
    raw = mm(normed_ref[...], pair_ref[...])
    raw_ref[...] = raw
    be[8 : 8 + rows, :] = raw
    lower = triangle(CHUNK, True).astype(BF16)
    left = left_half(CHUNK)
    lane = lax.broadcasted_iota(I32, (CHUNK, LANES), 1)
    for at in range(0, rows, CHUNK):
        here = slice(at, at + CHUNK)
        for lanes in (slice(0, STATE), slice(STATE, 2 * STATE)):
            pb = conv(be, btaps_ref, bbias_ref, at, CHUNK, lanes)
            bcs_ref[here, lanes] = pb * sigmoid(pb)
        step = softplus(step_ref[here, :] + head_ref[0:1, :])
        cum = summed_by(lower, -step * jnp.exp(head_ref[1:2, :]))
        sc_ref[here, :] = jnp.where(lane < HALF, step, pltpu.roll(cum, HALF, 1))
        end = cum[CHUNK - 1 : CHUNK, :]
        fading = step * jnp.exp(end - cum)
        keep = spread(rows8(jnp.exp(end)), channels)
        bt2 = halves(bcs_ref[here, :STATE].T)
        for pair in range(channels // LANES):
            lanes = slice(pair * LANES, (pair + 1) * LANES)
            p = conv(xe, taps_ref, bias_ref, at, CHUNK, lanes)
            xs = p * sigmoid(p)
            xs_ref[here, lanes] = xs
            weighted = halves(xs * spread_pair(fading, pair, left))
            state[:, lanes] = keep[0:1, lanes] * state[:, lanes] + dot3(bt2, weighted)
        total[...] += rows8(end)
    xe[0:8, :] = xe[rows : rows + 8, :]
    be[0:8, :] = be[rows : rows + 8, :]

    @pl.when(c == pl.num_programs(1) - 1)
    def _():
        end_ref[0:STATE, :] = state[...]
        end_ref[STATE : STATE + 8, :] = spread(jnp.exp(total[...]), channels)


def mix_kernel(
    meta_ref, xs_ref, bcs_ref, sc_ref, start_ref, gate_ref, gh_ref, chan_ref,
    mixed_ref, red_ref, states_ref, final_ref, state,
):
    c, rows = pl.program_id(1), xs_ref.shape[0]
    channels = xs_ref.shape[1]

    @pl.when(c == 0)
    def _():
        state[...] = start_ref[...]

    lower = triangle(CHUNK, True)
    left = left_half(CHUNK)
    zero = jnp.zeros((CHUNK, LANES), BF16)
    for at in range(0, rows, CHUNK):
        here = slice(at, at + CHUNK)
        entering = state[...]
        states_ref[at // CHUNK] = entering
        sc = sc_ref[here, :]
        sc_t = sc.T
        b2, c2 = halves(bcs_ref[here, :STATE]), halves(bcs_ref[here, STATE:])
        bt2 = halves(bcs_ref[here, :STATE].T)
        scores = dot3_t(c2, b2)
        carried = dot3(c2, halves(entering))
        end_full = spread(rows8(pltpu.roll(sc, HALF, 1)[CHUNK - 1 : CHUNK, :]), channels)
        sq = jnp.zeros((CHUNK, LANES), F32)
        dt = jnp.zeros((CHUNK, LANES), F32)
        for pair in range(channels // LANES):
            lanes = slice(pair * LANES, (pair + 1) * LANES)
            xs = xs_ref[here, lanes]
            weighted = xs * spread_pair(sc, pair, left)
            high, low = halves(weighted)
            stacked, columns = [], []
            for h in (HALF + 2 * pair, HALF + 2 * pair + 1):
                column = jnp.broadcast_to(sc[:, h : h + 1], (CHUNK, LANES))
                columns.append(column)
                mixing = jnp.where(lower, jnp.exp(column - sc_t[h : h + 1, :]), 0.0) * scores
                stacked.append(jnp.concatenate(halves(mixing), axis=1))
            right = jnp.concatenate(
                [jnp.concatenate([high, low], axis=1), jnp.concatenate([high, zero], axis=1)], axis=0
            )
            out = mm(jnp.concatenate(stacked, axis=0), right)
            out = out[:, :LANES] + out[:, LANES:]
            cum_full = jnp.where(left, columns[0], columns[1])
            mixed = (
                jnp.where(left, out[:CHUNK], out[CHUNK:])
                + carried[:, lanes] * jnp.exp(cum_full)
                + chan_ref[0:1, lanes] * xs
            )
            mixed_ref[here, lanes] = mixed
            gate = gate_ref[here, lanes]
            gated = mixed * (gate * sigmoid(gate))
            sq = sq + gated * gated
            dt = dt + gated * (gh_ref[here, lanes] * chan_ref[1:2, lanes])
            tail = end_full[0:1, lanes]
            later = halves(weighted * jnp.exp(tail - cum_full))
            state[:, lanes] = jnp.exp(tail) * state[:, lanes] + dot3(bt2, later)
        row = lax.broadcasted_iota(I32, (8, CHUNK), 0)
        red_ref[:, here] = jnp.where(row == 0, row_sums(sq), row_sums(dt))

    @pl.when(c == pl.num_programs(1) - 1)
    def _():
        final_ref[...] = state[...]


def gate_back_kernel(
    meta_ref, mixed_ref, gate_ref, gh_ref, row_ref, bcs_ref, sc_ref, chan_ref,
    hidden_ref, ggate_ref, dy_ref, gend_ref, acc_ref, peak_ref, grad, total,
):
    c, rows = pl.program_id(1), mixed_ref.shape[0]
    channels = mixed_ref.shape[1]

    @pl.when(c == 0)
    def _():
        grad[...] = jnp.zeros_like(grad)
        total[...] = jnp.zeros_like(total)

    @pl.when((c == 0) & (pl.program_id(0) == 0))
    def _():
        acc_ref[...] = jnp.zeros_like(acc_ref)
        peak_ref[...] = jnp.zeros_like(peak_ref)

    left = left_half(CHUNK)
    for at in reversed(range(0, rows, CHUNK)):
        here = slice(at, at + CHUNK)
        cum = pltpu.roll(sc_ref[here, :], HALF, 1)
        ct2 = halves(bcs_ref[here, STATE:].T)
        keep = spread(rows8(jnp.exp(cum[CHUNK - 1 : CHUNK, :])), channels)
        grown = jnp.exp(cum)
        squares, dots = as_column(row_ref[0:1, here]), as_column(row_ref[1:2, here])
        r = lax.rsqrt(squares * (1.0 / INNER) + EPSILON)
        pull = r * r * r * dots * (1.0 / INNER)
        for pair in range(channels // LANES):
            lanes = slice(pair * LANES, (pair + 1) * LANES)
            mixed, gate, gh = mixed_ref[here, lanes], gate_ref[here, lanes], gh_ref[here, lanes]
            out_gain = chan_ref[1:2, lanes]
            sig = sigmoid(gate)
            silu = gate * sig
            gated = mixed * silu
            normal = gated * r
            hidden_ref[here, lanes] = (normal * out_gain).astype(BF16)
            acc_ref[:, lanes] += fold8(gh * normal)
            grad_gated = r * (gh * out_gain) - gated * pull
            dy = grad_gated * silu
            dy_ref[here, lanes] = dy
            ggate = grad_gated * mixed * (sig * (1.0 + gate * (1.0 - sig)))
            ggate_ref[here, lanes] = ggate.astype(BF16)
            peak_ref[:, lanes] = jnp.maximum(peak_ref[:, lanes], jnp.maximum(peak8(ggate), peak8(dy)))
            grad[:, lanes] = keep[0:1, lanes] * grad[:, lanes] + dot3(
                ct2, halves(dy * spread_pair(grown, pair, left))
            )
        total[...] += rows8(cum[CHUNK - 1 : CHUNK, :])

    @pl.when(c == pl.num_programs(1) - 1)
    def _():
        gend_ref[0:STATE, :] = grad[...]
        gend_ref[STATE : STATE + 8, :] = spread(jnp.exp(total[...]), channels)


def state_back_kernel(
    meta_ref, x_ref, xprev_ref, xhalo_ref, bcs_ref, sc_ref, step_ref, dy_ref, mixed_ref, states_ref, final_ref,
    gin_ref, ggate_ref, taps_ref, bias_ref, head_ref, chan_ref, expand_ref,
    gp_ref, dbc_ref, tail_ref, first_ref, acc_ref, hacc_ref,
    xe, ge, grad, flux, wide, wlow, dhigh, dlow, sums,
):
    c, rows = pl.program_id(1), x_ref.shape[0]
    blocks = pl.num_programs(1)
    channels = x_ref.shape[1]
    expand = expand_ref[...]

    @pl.when((c == 0) & (pl.program_id(0) == 0))
    def _():
        acc_ref[...] = jnp.zeros_like(acc_ref)
        hacc_ref[...] = jnp.zeros_like(hacc_ref)

    @pl.when(c == 0)
    def _():
        grad[...] = gin_ref[...]
        ending = per_head(fold8(grad[...] * final_ref[...]), expand)
        flux[...] = rows8(jnp.sum(ending, axis=0, keepdims=True))
        ge[rows : rows + 8, :] = jnp.zeros((8, channels), F32)

    @pl.when(c != 0)
    def _():
        ge[rows : rows + 8, :] = ge[0:8, :]

    @pl.when(c == blocks - 1)
    def _():
        xe[0:8, :] = xhalo_ref[...]

    @pl.when(c != blocks - 1)
    def _():
        xe[0:8, :] = xprev_ref[...]

    xe[8 : 8 + rows, :] = x_ref[...]
    gp_ref[:, :channels] = ggate_ref[...]
    upper = triangle(CHUNK, False)
    left = left_half(CHUNK)
    zero = jnp.zeros((CHUNK, LANES), BF16)
    turn = lambda value: pltpu.roll(value.astype(F32), HEAD_DIM, 1).astype(BF16)
    for at in reversed(range(0, rows, CHUNK)):
        here = slice(at, at + CHUNK)
        sc = sc_ref[here, :]
        sc_t = sc.T
        cum = pltpu.roll(sc, HALF, 1)
        end_full = spread(rows8(cum[CHUNK - 1 : CHUNK, :]), channels)
        b2, c2 = halves(bcs_ref[here, :STATE]), halves(bcs_ref[here, STATE:])
        ct2 = halves(bcs_ref[here, STATE:].T)
        scores_t = dot3_t(b2, c2)
        leaving2 = halves(grad[...])
        pulled = dot3(b2, leaving2)
        dscores_t = jnp.zeros((CHUNK, CHUNK), F32)
        for pair in range(channels // LANES):
            lanes = slice(pair * LANES, (pair + 1) * LANES)
            p = conv(xe, taps_ref, bias_ref, at, CHUNK, lanes)
            sig = sigmoid(p)
            xs = p * sig
            slope = sig * (1.0 + p * (1.0 - sig))
            step_full = spread_pair(sc, pair, left)
            weighted = xs * step_full
            wh, wl = halves(weighted)
            dy = dy_ref[here, lanes]
            dh, dl = halves(dy)
            turned_wh, turned_wl, turned_dh = turn(wh), turn(wl), turn(dh)
            w_rows = (
                jnp.concatenate([jnp.where(left, wh, turned_wl), jnp.where(left, wh, zero)], axis=1),
                jnp.concatenate([jnp.where(left, turned_wh, wl), jnp.where(left, zero, wh)], axis=1),
            )
            d_rows = (
                jnp.concatenate([jnp.where(left, dh, turned_dh), dl], axis=1),
                jnp.concatenate([jnp.where(left, turned_dh, dh), dl], axis=1),
            )
            stacked, columns = [], []
            for side, h in enumerate((HALF + 2 * pair, HALF + 2 * pair + 1)):
                column = jnp.broadcast_to(sc[:, h : h + 1], (CHUNK, LANES))
                columns.append(column)
                kern = jnp.where(upper, jnp.exp(sc_t[h : h + 1, :] - column), 0.0)
                dscores_t = dscores_t + kern * mm(w_rows[side], d_rows[side], 1, 1)
                stacked.append(jnp.concatenate(halves(kern * scores_t), axis=1))
            right = jnp.concatenate(
                [jnp.concatenate([dh, dl], axis=1), jnp.concatenate([dh, zero], axis=1)], axis=0
            )
            out = mm(jnp.concatenate(stacked, axis=0), right)
            out = out[:, :LANES] + out[:, LANES:]
            cum_full = jnp.where(left, columns[0], columns[1])
            fade = jnp.exp(end_full[0:1, lanes] - cum_full)
            dxw = jnp.where(left, out[:CHUNK], out[CHUNK:]) + pulled[:, lanes] * fade
            grad_xs = step_full * dxw + chan_ref[0:1, lanes] * dy
            wide[:, lanes], wlow[:, lanes] = halves(weighted * fade)
            gh, gl = halves(dy * jnp.exp(cum_full))
            dhigh[:, lanes], dlow[:, lanes] = gh, gl
            keep = jnp.exp(end_full[0:1, lanes])
            grad[:, lanes] = keep * grad[:, lanes] + dot3(ct2, (gh, gl))
            sums[0:CHUNK, lanes] = xs * dxw
            sums[CHUNK:, lanes] = dy * mixed_ref[here, lanes] - xs * grad_xs
            grad_p = grad_xs * slope
            ge[here, lanes] = grad_p
            for k in range(CONV):
                acc_ref[8 * k : 8 * k + 8, lanes] += fold8(grad_p * xe[at + 5 + k : at + 5 + k + CHUNK, lanes])
            acc_ref[32:40, lanes] += fold8(grad_p)
            acc_ref[40:48, lanes] += fold8(dy * xs)
            raw = conv_back(ge, taps_ref, at, CHUNK, lanes)
            gp_ref[here, channels + pair * LANES : channels + (pair + 1) * LANES] = raw.astype(BF16)
            if at == rows - CHUNK:
                tail_ref[:, lanes] = raw[CHUNK - 8 :, :]
        entering2 = halves(states_ref[at // CHUNK])
        dscores2 = halves(dscores_t)
        dscores_back = halves(dscores_t.T)
        dbc_ref[here, :STATE] = dot3(dscores2, c2) + dot3_t((wide[...], wlow[...]), leaving2)
        dbc_ref[here, STATE:] = dot3(dscores_back, b2) + dot3_t((dhigh[...], dlow[...]), entering2)
        both = per_head(sums[...], expand)
        grad_rate = summed_by(upper.astype(BF16), both[CHUNK:]) + flux[0:1, :]
        flux[...] = rows8(grad_rate[0:1, :])
        rate_of = jnp.exp(head_ref[1:2, :])
        grad_step = both[:CHUNK] - rate_of * grad_rate
        grad_raw = grad_step * sigmoid(step_ref[here, :] + head_ref[0:1, :])
        hacc_ref[0:8, :] += fold8(grad_raw)
        hacc_ref[8:16, :] += fold8(-rate_of * jnp.where(lax.broadcasted_iota(I32, sc.shape, 1) < HALF, sc, 0.0) * grad_rate)
        gp_ref[here, 2 * channels :] = grad_raw.astype(BF16)

    @pl.when(c == blocks - 1)
    def _():
        first_ref[...] = ge[0:8, :]


def pair_back_kernel(
    meta_ref, raw_ref, halo_ref, g_ref, taps_ref, bias_ref, out_ref, tail_ref, first_ref, acc_ref, xe, ge
):
    length, channels = raw_ref.shape

    @pl.when(pl.program_id(0) == 0)
    def _():
        acc_ref[...] = jnp.zeros_like(acc_ref)

    xe[0:8, :] = halo_ref[...]
    xe[8 : 8 + length, :] = raw_ref[...]
    ge[length : length + 8, :] = jnp.zeros((8, channels), F32)
    for at in range(0, length, CHUNK):
        here = slice(at, at + CHUNK)
        for half in range(2):
            lanes = slice(half * STATE, (half + 1) * STATE)
            p = conv(xe, taps_ref, bias_ref, at, CHUNK, lanes)
            sig = sigmoid(p)
            grad_p = g_ref[here, lanes] * (sig * (1.0 + p * (1.0 - sig)))
            ge[here, lanes] = grad_p
            for k in range(CONV):
                acc_ref[8 * k : 8 * k + 8, lanes] += fold8(grad_p * xe[at + 5 + k : at + 5 + k + CHUNK, lanes])
            acc_ref[32:40, lanes] += fold8(grad_p)
    for at in range(0, length, CHUNK):
        for lanes in (slice(0, STATE), slice(STATE, 2 * STATE)):
            raw = conv_back(ge, taps_ref, at, CHUNK, lanes)
            out_ref[at : at + CHUNK, lanes] = raw.astype(BF16)
            if at == length - CHUNK:
                tail_ref[:, lanes] = raw[CHUNK - 8 :, :]
    first_ref[...] = ge[0:8, :]


def finish_kernel(meta_ref, gn_ref, u_ref, branch_ref, gbc_ref, weight_ref, gain_ref, *refs):
    out_ref, acc_ref = refs[-2:]

    @pl.when((pl.program_id(1) == 0) & (pl.program_id(0) == 0))
    def _():
        acc_ref[...] = jnp.zeros_like(acc_ref)

    u = u_ref[...].astype(F32)
    scale = lax.rsqrt(jnp.mean(u * u, axis=-1, keepdims=True) + EPSILON)
    grad = gn_ref[...] + mm(gbc_ref[...], weight_ref[...], 1, 1)
    normal = u * scale
    acc_ref[...] += fold8(grad * normal)
    w = grad * gain_ref[...]
    pull = scale * jnp.mean(w * normal, axis=-1, keepdims=True)
    out_ref[...] = scale * w - normal * pull + branch_ref[...].astype(F32)


def place_kernel(meta_ref, own_ref, got_ref, *refs, takes_at):
    out_ref = refs[-1]
    takes = meta_ref[takes_at] == 1

    @pl.when(takes)
    def _():
        out_ref[...] = got_ref[...]

    @pl.when(jnp.logical_not(takes))
    def _():
        out_ref[...] = own_ref[...]


SHAPE = jax.ShapeDtypeStruct


def whole(shape):
    return pl.BlockSpec(shape, lambda s, c, meta: (0,) * len(shape))


def per_seq(rows, width):
    return pl.BlockSpec((None, rows, width), lambda s, c, meta: (s, 0, 0))


def forward_rows(width, column):
    return pl.BlockSpec((None, ROWS, width), lambda s, c, meta: (s, c, column))


def constants(lengths, step_bias, decay_log, skip_gain, out_gain, slots):
    seqs, channels = lengths.shape[0], out_gain.shape[0]
    row = lambda value: value[None]
    smem = pl.BlockSpec(memory_space=pltpu.SMEM)
    vmem = pl.BlockSpec(memory_space=pltpu.VMEM)
    return pl.pallas_call(
        functools.partial(constants_kernel, slots=slots),
        in_specs=[smem] + [vmem] * 4,
        out_specs=[smem, vmem, vmem, vmem],
        out_shape=[
            SHAPE((2 * seqs + 1,), jnp.int32), SHAPE((8, LANES), F32), SHAPE((8, channels), F32),
            SHAPE((LANES, channels), BF16),
        ],
        name="constants",
    )(lengths, row(step_bias), row(decay_log), row(skip_gain), row(out_gain))


def project(order, meta, residual_in, cotangent, gain, gate, x, step, out, first, count):
    seqs, slots, width = residual_in.shape
    channels = gate.shape[1]
    rows = 256
    placed = pl.BlockSpec((None, rows, width), lambda s, c, meta: (meta[s + first], c, 0))
    plain = lambda wide: pl.BlockSpec((None, rows, wide), lambda s, c, meta: (s, c, 0))
    wide = 2 * channels + LANES
    return order.call(
        functools.partial(project_kernel, first=first),
        (residual_in, cotangent, gain, gate, x, step, out),
        meta=meta,
        grid=(count, slots // rows),
        in_specs=[placed, placed] + [whole(a.shape) for a in (gain, gate, x, step, out)],
        out_specs=[plain(width), plain(width), plain(wide), plain(channels)],
        out_shape=[
            SHAPE((count, slots, width), BF16), SHAPE((count, slots, width), BF16),
            SHAPE((count, slots, wide), F32), SHAPE((count, slots, channels), F32),
        ],
        flops=2 * count * slots * width * (wide + channels),
        moved=count * slots * (width * 8 + wide * 4),
        name="project",
    )


def edge_halos(order, meta, before, gain, x, pair):
    seqs = before.shape[0]
    operands = (before, gain, x, pair)
    shapes = [(seqs, 8, x.shape[1]), (seqs, 8, pair.shape[1])]
    return order.call(
        edge_kernel,
        operands,
        meta=meta,
        grid=(1, 1),
        in_specs=[whole(a.shape) for a in operands],
        out_specs=[whole(a) for a in shapes],
        out_shape=[SHAPE(a, F32) for a in shapes],
        flops=1e8,
        moved=4e6,
        name="edge_halos",
    )


def local_states(order, meta, proj, normed, pair, halo_x, halo_bc, taps, bias, btaps, bbias, head, first, channels):
    count, slots, _ = proj.shape
    placed = lambda width: pl.BlockSpec((None, 8, width), lambda s, c, meta: (meta[first + s], 0, 0))
    return order.call(
        local_state_kernel,
        (proj, halo_x, normed, pair, halo_bc, proj, taps, bias, btaps, bbias, head),
        meta=meta,
        grid=(count, slots // ROWS),
        in_specs=[
            forward_rows(channels, 1), placed(channels), forward_rows(normed.shape[2], 0), whole(pair.shape),
            placed(2 * STATE),
            forward_rows(LANES, 2 * channels // LANES), whole(taps.shape), whole(bias.shape), whole(btaps.shape),
            whole(bbias.shape), whole(head.shape),
        ],
        out_specs=[
            forward_rows(channels, 0), forward_rows(2 * STATE, 0), forward_rows(2 * STATE, 0),
            forward_rows(LANES, 0), per_seq(STATE + 8, channels),
        ],
        out_shape=[
            SHAPE((count, slots, channels), F32), SHAPE((count, slots, 2 * STATE), F32),
            SHAPE((count, slots, 2 * STATE), F32),
            SHAPE((count, slots, LANES), F32), SHAPE((count, STATE + 8, channels), F32),
        ],
        scratch=[
            pltpu.VMEM((ROWS + 8, channels), F32), pltpu.VMEM((ROWS + 8, 2 * STATE), F32),
            pltpu.VMEM((STATE, channels), F32), pltpu.VMEM((8, LANES), F32),
        ],
        flops=count * 4e9,
        moved=count * slots * channels * 8,
        name="local_states",
    )


def mix(order, meta, xs, bcs, sc, start, proj, grad_hidden, chan):
    count, slots, channels = xs.shape
    chunks = slots // CHUNK
    return order.call(
        mix_kernel,
        (xs, bcs, sc, start, proj, grad_hidden, chan),
        meta=meta,
        grid=(count, slots // ROWS),
        in_specs=[
            forward_rows(channels, 0), forward_rows(2 * STATE, 0), forward_rows(LANES, 0),
            per_seq(STATE, channels),
            forward_rows(channels, 0), forward_rows(channels, 0), whole(chan.shape),
        ],
        out_specs=[
            forward_rows(channels, 0), pl.BlockSpec((None, 8, ROWS), lambda s, c, meta: (s, 0, c)),
            pl.BlockSpec((None, ROWS // CHUNK, STATE, channels), lambda s, c, meta: (s, c, 0, 0)),
            per_seq(STATE, channels),
        ],
        out_shape=[
            SHAPE((count, slots, channels), F32), SHAPE((count, 8, slots), F32),
            SHAPE((count, chunks, STATE, channels), F32), SHAPE((count, STATE, channels), F32),
        ],
        scratch=[pltpu.VMEM((STATE, channels), F32)],
        flops=count * 6e9,
        moved=count * slots * channels * 20,
        name="mix",
    )


def gate_back(order, meta, mixed, proj, grad_hidden, rows, bcs, sc, chan):
    count, slots, channels = mixed.shape
    chunks = slots // ROWS
    row = lambda width, column: pl.BlockSpec(
        (None, ROWS, width), lambda s, c, meta: (s, chunks - 1 - c, column)
    )
    return order.call(
        gate_back_kernel,
        (mixed, proj, grad_hidden, rows, bcs, sc, chan),
        meta=meta,
        grid=(count, chunks),
        in_specs=[
            row(channels, 0), row(channels, 0), row(channels, 0),
            pl.BlockSpec((None, 8, ROWS), lambda s, c, meta: (s, 0, chunks - 1 - c)), row(2 * STATE, 0),
            row(LANES, 0), whole(chan.shape),
        ],
        out_specs=[
            row(channels, 0), row(channels, 0), row(channels, 0), per_seq(STATE + 8, channels),
            whole((8, channels)), whole((8, channels)),
        ],
        out_shape=[
            SHAPE((count, slots, channels), BF16), SHAPE((count, slots, channels), BF16),
            SHAPE((count, slots, channels), F32), SHAPE((count, STATE + 8, channels), F32),
            SHAPE((8, channels), F32), SHAPE((8, channels), F32),
        ],
        scratch=[pltpu.VMEM((STATE, channels), F32), pltpu.VMEM((8, LANES), F32)],
        flops=count * 4e9,
        moved=count * slots * channels * 20,
        name="gate_back",
    )


def state_back(
    order, meta, at, first, proj, halo_x, bcs, sc, dy, mixed, states, final, grad_in, grad_gate, taps, bias, head, chan, expand
):
    _, slots, channels = mixed.shape
    chunks = slots // ROWS
    tiles = ROWS // 8
    row = lambda width, column, s=at: pl.BlockSpec(
        (None, ROWS, width), lambda _, c, meta: (s, chunks - 1 - c, column)
    )
    only = lambda rows, width, s=at: pl.BlockSpec((None, rows, width), lambda _, c, meta: (s, 0, 0))
    before = pl.BlockSpec(
        (None, 8, channels), lambda _, c, meta: (at, jnp.maximum((chunks - 1 - c) * tiles - 1, 0), 1)
    )
    tail = pl.BlockSpec((None, None, 8, channels), lambda _, c, meta: (0, chunks - 1 - c, 0, 0))
    return order.call(
        state_back_kernel,
        (
            proj, proj, halo_x, bcs, sc, proj, dy, mixed, states, final, grad_in, grad_gate, taps, bias, head, chan,
            expand,
        ),
        meta=meta,
        grid=(1, chunks),
        in_specs=[
            row(channels, 1), before,
            pl.BlockSpec((None, 8, channels), lambda _, c, meta: (meta[first + at], 0, 0)),
            row(2 * STATE, 0), row(LANES, 0),
            row(LANES, 2 * channels // LANES), row(channels, 0), row(channels, 0),
            pl.BlockSpec((None, ROWS // CHUNK, STATE, channels), lambda _, c, meta: (at, chunks - 1 - c, 0, 0)),
            only(STATE, channels),
            only(STATE, channels),
            row(channels, 0),
            whole(taps.shape), whole(bias.shape), whole(head.shape), whole(chan.shape), whole(expand.shape),
        ],
        out_specs=[
            row(2 * channels + LANES, 0, 0), row(2 * STATE, 0, 0), tail, only(8, channels, 0),
            whole((48, channels)), whole((16, LANES)),
        ],
        out_shape=[
            SHAPE((1, slots, 2 * channels + LANES), BF16), SHAPE((1, slots, 2 * STATE), F32),
            SHAPE((1, chunks, 8, channels), F32), SHAPE((1, 8, channels), F32),
            SHAPE((48, channels), F32), SHAPE((16, LANES), F32),
        ],
        scratch=[
            pltpu.VMEM((ROWS + 8, channels), F32), pltpu.VMEM((ROWS + 8, channels), F32),
            pltpu.VMEM((STATE, channels), F32), pltpu.VMEM((8, LANES), F32),
            pltpu.VMEM((CHUNK, channels), BF16), pltpu.VMEM((CHUNK, channels), BF16),
            pltpu.VMEM((CHUNK, channels), BF16), pltpu.VMEM((CHUNK, channels), BF16),
            pltpu.VMEM((2 * CHUNK, channels), F32),
        ],
        flops=12e9,
        moved=slots * channels * 24,
        name="state_back",
    )


def pair_back(order, meta, first, raw, halo, grad, taps, bias):
    count, slots, channels = raw.shape
    placed = pl.BlockSpec((None, 8, channels), lambda s, c, meta: (meta[first + s], 0, 0))
    return order.call(
        pair_back_kernel,
        (raw, halo, grad, taps, bias),
        meta=meta,
        grid=(count, 1),
        in_specs=[
            per_seq(slots, channels), placed, per_seq(slots, channels), whole(taps.shape), whole(bias.shape),
        ],
        out_specs=[
            per_seq(slots, channels), per_seq(8, channels), per_seq(8, channels), whole((40, channels)),
        ],
        out_shape=[
            SHAPE((count, slots, channels), BF16), SHAPE((count, 8, channels), F32),
            SHAPE((count, 8, channels), F32), SHAPE((40, channels), F32),
        ],
        scratch=[pltpu.VMEM((slots + 8, channels), F32), pltpu.VMEM((slots + 8, channels), F32)],
        flops=count * 1e9,
        moved=count * slots * channels * 10,
        name="pair_back",
    )


def finish(order, meta, grad_normed, residual_in, branch, gbc, weight, gain, at, local, target):
    seqs, slots, width = residual_in.shape
    rows = 128
    placed = pl.BlockSpec((None, rows, width), lambda s, c, meta: (meta[at], c, 0))
    fixed = lambda where, wide: pl.BlockSpec((None, rows, wide), lambda s, c, meta: (where, c, 0))
    extra = () if target is None else (target,)
    return order.call(
        finish_kernel,
        (grad_normed, residual_in, branch, gbc, weight, gain) + extra,
        meta=meta,
        grid=(1, slots // rows),
        in_specs=[
            fixed(0, width), placed, fixed(local, width), fixed(local, gbc.shape[2]),
            whole(weight.shape), whole(gain.shape),
        ] + [ANYWHERE] * len(extra),
        out_specs=[placed, whole((8, width))],
        out_shape=[SHAPE((seqs, slots, width), F32), SHAPE((8, width), F32)],
        aliases={7: 0} if extra else None,
        flops=1e9,
        moved=slots * width * 14,
        name="finish",
    )


def place(order, meta, own, got, at, seqs, target):
    count, slots, width = own.shape
    rows = 256
    plain = pl.BlockSpec((None, rows, width), lambda s, c, meta: (s, c, 0))
    placed = pl.BlockSpec((None, rows, width), lambda s, c, meta: (meta[at + s], c, 0))
    extra = () if target is None else (target,)
    return order.call(
        functools.partial(place_kernel, takes_at=2 * seqs),
        (own, got) + extra,
        meta=meta,
        grid=(count, slots // rows),
        in_specs=[plain, plain] + [ANYWHERE] * len(extra),
        out_specs=[placed],
        out_shape=[SHAPE((seqs, slots, width), own.dtype)],
        aliases={3: 0} if extra else None,
        flops=1e6,
        moved=count * slots * width * 6,
        name="place",
    )[0]


class Running:
    def __init__(self, order, steps):
        self.order, self.steps, self.value, self.ended = order, steps, None, False
        self.advance()

    def advance(self, times=1):
        for _ in range(times):
            if self.ended:
                return self
            try:
                sent = next(self.steps)
                self.order.before_next(*sent)
            except StopIteration as stop:
                self.value, self.ended = stop.value, True
        return self

    def end(self):
        while not self.ended:
            self.advance()
        return self.value


def line_sum(order, part, axis, finish, choose=True):
    count, mine = lax.axis_size(axis), lax.axis_index(axis)
    if count % 2:
        done = finish(lax.psum(part.astype(F32), axis))
        return done if choose else (done, done)
    middle = count // 2
    send = lambda value, pairs: lax.ppermute(value, axis, pairs)
    plus = lambda a, b: order.tie(a.astype(F32) + b.astype(F32))
    for k in range(middle - 1):
        pairs = [(k, k + 1), (count - 1 - k, count - 2 - k)]
        got = send(part, pairs)
        yield (part,)
        part = plus(part, got).astype(part.dtype)
    got = send(part, [(middle - 1, middle), (middle, middle - 1)])
    yield (part,)
    done = finish(plus(part, got))
    for k in range(middle - 1, 0, -1):
        got = send(done, [(k, k - 1), (count - 1 - k, count - k)])
        yield (done,)
        if k == 1 and not choose:
            return done, got
        takes = (mine == k - 1) | (mine == count - k)
        done = order.tie(jnp.where(takes, got, done))
    return done if choose else (done, done)


def crossed(order, value, axis, join):
    count = lax.axis_size(axis)
    pairs = lambda distance: [(i, (i + distance) % count) for i in range(count)]
    got = [lax.ppermute(value, axis, pairs(distance)) for distance in range(1, count)]
    yield (value,)
    for other in got:
        value = join(value, other)
    return order.tie(value)


def bits_of(axis):
    size = lax.axis_size(axis)
    assert size & (size - 1) == 0
    return [1 << k for k in range(size.bit_length() - 1)]


def flipped(value, axis, bit):
    return lax.ppermute(value, axis, [(i, i ^ bit) for i in range(lax.axis_size(axis))])


def pack(state, decay):
    return jnp.concatenate([state, jnp.broadcast_to(decay, decay.shape[:-2] + (8, decay.shape[-1]))], axis=-2)


def carried(order, payload, axis, backward):
    mine, size = lax.axis_index(axis), lax.axis_size(axis)
    steps = bits_of(axis)
    odd = (mine & 1) == 1
    own = jnp.where(odd, payload[1], payload[0])
    give = jnp.where(odd, payload[0], payload[1])
    got = flipped(give, axis, 1)
    yield (give,)
    is_first = odd if backward else jnp.logical_not(odd)
    one, two = jnp.where(is_first, own, got), jnp.where(is_first, got, own)
    one_decay, two_decay = order.tie(one[STATE : STATE + 1]), order.tie(two[STATE : STATE + 1])
    state = two_decay * one[:STATE] + two[:STATE]
    decay = one_decay * two_decay
    entering, through = jnp.zeros_like(state), jnp.ones_like(decay)
    for bit in steps[1:]:
        later = ((mine & bit) == 0) if backward else ((mine & bit) != 0)
        last = bit == steps[-1]
        pairs = [(i, i ^ bit) for i in range(size) if not last or bool(i & bit) == backward]
        sent = pack(state, decay)
        got = lax.ppermute(sent, axis, pairs)
        yield (sent,)
        got_state, got_decay = got[:STATE], order.tie(got[STATE : STATE + 1])
        through = order.tie(through)
        entering = jnp.where(later, through * got_state + entering, entering)
        through = jnp.where(later, got_decay * through, through)
        if not last:
            state = jnp.where(later, decay * got_state + state, got_decay * state + got_state)
            decay = decay * got_decay
    second = one_decay * entering + one[:STATE]
    mine_now, other_now = jnp.where(is_first, entering, second), jnp.where(is_first, second, entering)
    back = flipped(other_now, axis, 1)
    yield (other_now,)
    return jnp.stack([jnp.where(odd, back, mine_now), jnp.where(odd, mine_now, back)])


def butterfly_sum(value, axis):
    for bit in bits_of(axis):
        value = value + flipped(value, axis, bit)
    return value


def gathered(order, value, axis):
    mine = lax.axis_index(axis)
    for bit in bits_of(axis):
        got = flipped(value, axis, bit)
        yield (value,)
        got = order.tie(got)
        value = jnp.where(
            (mine & bit) == 0, jnp.concatenate([value, got], axis=1), jnp.concatenate([got, value], axis=1)
        )
    return value


def shifted(block, axis, distance):
    devices = range(lax.axis_size(axis))
    route = [(i - distance, i) for i in devices if i - distance in devices]
    return lax.ppermute(block, axis, route)


BRANCH_SCALE = 64.0


def pad_lanes(value, width):
    return jnp.pad(value, [(0, 0)] * (value.ndim - 1) + [(0, width - value.shape[-1])])


def edge_terms(halo, taps):
    ext = jnp.concatenate([jnp.zeros_like(halo), halo], axis=1)
    return sum(taps[CONV - 1 - j] * ext[:, j : j + 8] for j in range(1, CONV))


def per_device(
    residual_in, lengths, norm_gain, gate_projection_weight, head_channels_weight, input_state_pair_weight,
    step_size_weight, x_taps, bc_taps, x_bias, bc_bias, step_bias, decay_log, skip_gain, out_gain,
    output_projection_weight, cotangent,
):
    seqs, slots, width = residual_in.shape
    channels = head_channels_weight.shape[1]
    own = input_state_pair_weight.shape[1]
    heads = step_size_weight.shape[1]
    head_at = lax.axis_index("head")
    count = seqs // GROUPS
    groups = range(GROUPS)
    dot = lambda spec, a, b: jnp.einsum(spec, a, b, preferred_element_type=F32)

    order = Order()
    run = lambda steps: Running(order, steps)

    meta, head, chan, expand = constants(lengths, step_bias, decay_log, skip_gain, out_gain, slots)
    places, limit = meta[:seqs], meta[seqs : 2 * seqs]
    slot = lax.iota(jnp.int32, slots)[:, None]

    before = shifted(residual_in[:, slots - 8 :], "seq", 1)
    pair_gather = run(gathered(order, input_state_pair_weight, "head"))
    taps_gather = run(
        gathered(order, jnp.pad(jnp.concatenate([bc_taps, bc_bias[None]], 0), ((0, 3), (0, 0))), "head")
    )
    step_weight = pad_lanes(step_size_weight, LANES)
    out_weight_t = output_projection_weight.T
    bias = x_bias[None]
    gain_row = norm_gain[None]

    normed, branch_grad, proj, bc_raw, xs, bcs, sc, grad_hidden = ([None] * GROUPS for _ in range(8))
    starts, partials, mixed, states, final, ends = ([None] * GROUPS for _ in range(6))
    hidden, grad_gate, dy, grad_ins, gain_acc, gate_peak = ([None] * GROUPS for _ in range(6))
    branches, sums_of = {}, {}

    def project_of(g):
        normed[g], branch_grad[g], proj[g], grad_hidden[g] = project(
            order, meta, residual_in, cotangent, gain_row, gate_projection_weight, head_channels_weight, step_weight,
            out_weight_t, g * count, count,
        )

    def states_of(g):
        xs[g], bc_raw[g], bcs[g], sc[g], ends[g] = local_states(
            order, meta, proj[g], normed[g], pair_weight, halo_x, halo_bc, x_taps, bias, bc_taps_all, bc_bias_all,
            head, g * count, channels,
        )
        starts[g] = run(carried(order, ends[g], "seq", False))

    def mix_of(g):
        mixed[g], sums, states[g], final[g] = mix(
            order, meta, xs[g], bcs[g], sc[g], starts[g].end(), proj[g], grad_hidden[g], chan
        )
        sums_of[g] = run(crossed(order, sums, "head", lambda a, b: a + b))

    def gate_of(g):
        hidden[g], grad_gate[g], dy[g], grad_end, gain_acc[g], gate_peak[g] = gate_back(
            order, meta, mixed[g], proj[g], grad_hidden[g], sums_of[g].end(), bcs[g], sc[g], chan
        )
        grad_ins[g] = run(carried(order, grad_end, "seq", True))

    def branch_of(s):
        g, i = divmod(s, count)
        branch = (dot("mq,qh->mh", hidden[g][i], output_projection_weight) * BRANCH_SCALE).astype(F16)
        u = lax.dynamic_index_in_dim(residual_in, places[s], 0, keepdims=False)
        done = lambda total: jnp.where(
            slot < limit[s], u.astype(F32) + total * (1.0 / BRANCH_SCALE), 0.0
        ).astype(BF16)
        branches[s] = run(line_sum(order, branch, "head", done, choose=False))

    def result_of(s, target):
        own_rows, got = branches[s].end()
        return place(order, meta, own_rows[None], got[None], s, seqs, target)

    gps, dbcs, tails, edges, accs, haccs = ({} for _ in range(6))
    parts, gbcs, baccs, gain_accs = {}, {}, [], []
    dbc_sums, fixes = {}, {}

    def peaks_of():
        largest = functools.reduce(jnp.maximum, [jnp.max(peak) for peak in gate_peak])
        return run(crossed(order, jnp.full((8, LANES), largest, F32), "head", jnp.maximum))

    def back_of(s):
        g, i = divmod(s, count)
        gps[s], dbcs[s], tails[s], edges[s], accs[s], haccs[s] = state_back(
            order, meta, i, g * count, proj[g], halo_x, bcs[g], sc[g], dy[g], mixed[g], states[g], final[g],
            grad_ins[g].end(), grad_gate[g], x_taps, bias, head, chan, expand,
        )

    def edges_of(g):
        mine = [g * count + i for i in range(count)]
        edge = jnp.concatenate([edges[s] for s in mine])
        fixes[g] = (shifted(edge, "seq", -1), jnp.concatenate([tails[s][:, -1] for s in mine]))
        order.before_next(edge)
        dbc_sums[g] = run(line_sum(order, jnp.concatenate([dbcs[s] for s in mine]), "head", lambda total: total))

    def fix_of(g):
        got, tail = fixes[g]
        fixed = order.tie(tail + edge_terms(got, x_taps)).astype(BF16)
        for i in range(count):
            s = g * count + i
            gps[s] = lax.dynamic_update_slice(gps[s][0], fixed[i], (slots - 8, channels))

    def part_of(s):
        part = (dot("gl,ol->go", gps[s], weight) * scale[0]).astype(F16)
        parts[s] = run(line_sum(order, part, "head", lambda total: total.astype(F16)))

    def pair_of(g):
        gbc, btail, bedge, bacc = pair_back(
            order, meta, g * count, bc_raw[g], halo_bc, dbc_sums[g].end(), bc_taps_all, bc_bias_all
        )
        baccs.append(bacc)
        gbcs[g] = (gbc, btail, shifted(bedge, "seq", -1))
        order.before_next(bedge)

    def pair_fix(g):
        gbc, btail, got = gbcs[g]
        fixed = order.tie(btail + edge_terms(got, bc_taps_all)).astype(BF16)
        gbcs[g] = lax.dynamic_update_slice(gbc, fixed, (0, slots - 8, 0))

    def finish_of(s, target):
        g, i = divmod(s, count)
        total = parts[s].end().astype(F32) * scale[1]
        target, gain = finish(
            order, meta, total[None], residual_in, branch_grad[g], gbcs[g], pair_weight, gain_row, s, i, target
        )
        gain_accs.append(gain)
        return target

    add = lambda terms: functools.reduce(lambda a, b: a + b, terms)
    tied_dots = lambda spec, pairs: order.tie(add([dot(spec, a, b) for a, b in pairs]))
    project_of(0)
    pair_gather.advance()
    taps_gather.advance()
    project_of(1)
    pair_weight = pair_gather.end()
    bc_taps_all, bc_bias_all = taps_gather.end()[:CONV], taps_gather.end()[CONV : CONV + 1]
    halo_x, halo_bc = edge_halos(order, meta, before, gain_row, head_channels_weight, pair_weight)
    states_of(0)
    order.fence()
    weight = jnp.concatenate([gate_projection_weight, head_channels_weight, order.tie(step_weight)], axis=1)
    order.before_next(weight)
    starts[0].advance()
    states_of(1)
    starts[0].advance()
    order.fence()
    starts[1].advance()
    order.fence()
    starts[0].advance()
    starts[1].advance()
    mix_of(0)
    starts[1].advance()
    mix_of(1)
    gate_of(0)
    branch_of(0)
    order.fence()
    grad_ins[0].advance()
    gate_of(1)
    grad_ins[0].advance()
    order.fence()
    branch_of(1)
    grad_ins[1].advance()
    order.fence()
    out_grad = tied_dots("yfx,yfw->xw", [(hidden[g], branch_grad[g]) for g in groups])
    order.before_next(out_grad)
    order.fence()
    grad_ins[0].advance()
    grad_ins[1].advance()
    branch_of(2)
    peak = peaks_of()
    back_of(0)
    grad_ins[1].advance()
    branches[0].advance()
    back_of(1)
    edges_of(0)
    branch_of(3)
    gate_grad = tied_dots("wji,wjr->ir", [(normed[g], grad_gate[g]) for g in groups])
    early = lax.psum((out_grad, gate_grad, order.tie(jnp.zeros((8, LANES), F32))), "seq")
    branches[1].advance()
    branches[0].advance()
    back_of(2)
    peak = jnp.maximum(peak.end()[0, 0], 1e-30)
    scale = 0.5 / peak, 2.0 * peak
    fix_of(0)
    part_of(0)
    branches[2].advance()
    branches[1].advance()
    back_of(3)
    edges_of(1)
    dbc_sums[0].advance()
    result = result_of(0, None)
    branches[3].advance()
    branches[2].advance()
    part_of(1)
    dbc_sums[0].advance()
    fix_of(1)
    part_of(2)
    result = result_of(1, result)
    branches[3].advance()
    parts[0].advance()
    pair_of(0)
    pair_fix(0)
    result = result_of(2, result)
    part_of(3)
    order.fence()
    grad_x_weight = tied_dots(
        "ji,jr->ir", [(normed[s // count][s % count], gps[s][..., channels : 2 * channels]) for s in range(seqs)]
    )
    grad_step_weight = tied_dots(
        "ji,jr->ir", [(normed[s // count][s % count], gps[s][..., 2 * channels :]) for s in range(seqs)]
    )
    order.before_next(grad_x_weight, grad_step_weight)
    order.fence()
    dbc_sums[1].advance()
    parts[1].advance()
    parts[0].advance()
    result = result_of(3, result)
    zero = order.tie(jnp.zeros((8, LANES), F32)) + jnp.clip(early[0][0, 0] + early[1][0, 0], -1.0, 1.0) * 0.0
    late = lax.psum((grad_x_weight, grad_step_weight, zero), "seq")
    parts[2].advance()
    parts[1].advance()
    dbc_sums[1].advance()
    grad_input = finish_of(0, None)
    parts[3].advance()
    parts[2].advance()
    pair_of(1)
    pair_fix(1)
    grad_pair = add(dot("wji,wjr->ir", normed[g], gbcs[g]) for g in groups)
    grad_own = lax.dynamic_slice(grad_pair, (0, head_at * own), (width, own))
    grad_input = finish_of(1, grad_input)
    parts[3].advance()
    grad_input = finish_of(2, grad_input)
    grad_input = finish_of(3, grad_input)
    acc = jnp.sum(add(accs.values()).reshape(6, 8, channels), axis=1)
    acc = jnp.concatenate([acc, jnp.sum(add(gain_acc), axis=0)[None]], axis=0)
    hacc = jnp.sum(add(haccs.values()).reshape(2, 8, LANES), axis=1)
    bacc = jnp.sum(add(baccs).reshape(5, 8, 2 * STATE), axis=1)
    flat = jnp.concatenate([acc.reshape(-1), hacc.reshape(-1), bacc.reshape(-1), grad_own.reshape(-1)])
    flat = butterfly_sum(flat.reshape(-1, LANES), "seq").reshape(-1)
    ends_at = [acc.size, acc.size + hacc.size, acc.size + hacc.size + bacc.size]
    acc, hacc, bacc, grad_own = (
        piece.reshape(like.shape) for piece, like in zip(jnp.split(flat, ends_at), (acc, hacc, bacc, grad_own))
    )
    bacc = lax.dynamic_slice(bacc, (0, head_at * own), (5, own))
    gain = butterfly_sum(jnp.sum(add(gain_accs), axis=0).reshape(-1, LANES), "seq").reshape(-1)
    return (
        result,
        grad_input,
        gain,
        early[1],
        late[0],
        grad_own,
        late[1][:, :heads],
        acc[:CONV],
        bacc[:CONV],
        acc[CONV],
        bacc[CONV],
        hacc[0, :heads],
        hacc[1, :heads],
        jnp.sum(acc[5].reshape(heads, HEAD_DIM), axis=1),
        acc[6],
        early[0],
    )


def solution(mesh):
    return jax.shard_map(
        per_device,
        mesh=mesh,
        in_specs=(
            P(None, "seq", None), P(), P(), P(None, "head"), P(None, "head"), P(None, "head"), P(None, "head"),
            P(None, "head"), P(None, "head"), P("head"), P("head"), P("head"), P("head"), P("head"), P("head"),
            P("head", None), P(None, "seq", None),
        ),
        out_specs=(
            P(None, "seq", None), P(None, "seq", None), P(), P(None, "head"), P(None, "head"), P(None, "head"),
            P(None, "head"), P(None, "head"), P(None, "head"), P("head"), P("head"), P("head"), P("head"),
            P("head"), P("head"), P("head", None),
        ),
        check_vma=False,
    )
```

```python
import functools

import jax
import jax.numpy as jnp
from jax import lax
from jax.experimental import pallas as pl
from jax.experimental.pallas import tpu as pltpu
from jax.sharding import PartitionSpec as P

HEAD_DIM = 64
STATE = 128
CONV = 4
INNER = 3072
CHUNK = 128
ROWS = 256
HALF = 64
LANES = 128
EPSILON = 1e-05
GROUPS = 2
F32 = jnp.float32
BF16 = jnp.bfloat16
F16 = jnp.float16
I32 = jnp.int32
VMEM_LIMIT = 60 * 1024 * 1024


def halves(value):
    high = value.astype(BF16)
    return high, (value - high.astype(F32)).astype(BF16)


def thirds(value):
    high = value.astype(BF16)
    rest = value - high.astype(F32)
    middle = rest.astype(BF16)
    return high, middle, (rest - middle.astype(F32)).astype(BF16)


def mm(a, b, ca=1, cb=0):
    return lax.dot_general(a, b, (((ca,), (cb,)), ((), ())), preferred_element_type=F32)


def dot3(a, b):
    return mm(jnp.concatenate([a[0], a[1]], axis=1), jnp.concatenate([b[0], b[0]], axis=0)) + mm(a[0], b[1])


def dot3_t(a, b):
    n = b[0].shape[0]
    wide = mm(a[0], jnp.concatenate([b[0], b[1]], axis=0), 1, 1)
    return wide[:, :n] + wide[:, n:] + mm(a[1], b[0], 1, 1)


def per_head(value, expand):
    high, low = halves(value)
    return mm(high, expand, 1, 1) + mm(low, expand, 1, 1)


def summed_by(matrix, value):
    out = None
    for part in thirds(value):
        term = mm(matrix, part)
        out = term if out is None else out + term
    return out


def rows8(row):
    return jnp.broadcast_to(row, (8, row.shape[-1]))


def fold8(value):
    return jnp.sum(value.reshape(value.shape[0] // 8, 8, value.shape[1]), axis=0)


def peak8(value):
    return jnp.max(jnp.abs(value).reshape(value.shape[0] // 8, 8, value.shape[1]), axis=0)


def left_half(rows):
    return lax.broadcasted_iota(jnp.int32, (rows, LANES), 1) < HEAD_DIM


def spread_pair(value, pair, left):
    h = 2 * pair
    return jnp.where(left, value[:, h : h + 1], value[:, h + 1 : h + 2])


def spread(value, channels):
    left = left_half(value.shape[0])
    return jnp.concatenate([spread_pair(value, j, left) for j in range(channels // LANES)], axis=1)


def softplus(value):
    small = jnp.exp(-jnp.abs(value))
    one = 1.0 + small
    log = jnp.where(one == 1.0, small, jnp.log(one) * (small / jnp.where(one == 1.0, 1.0, one - 1.0)))
    return jnp.maximum(value, 0.0) + log


def sigmoid(value):
    return 1.0 / (1.0 + jnp.exp(-value))


def conv(ext_ref, taps_ref, bias_ref, start, length, lanes):
    summed = bias_ref[0:1, lanes] + taps_ref[0:1, lanes] * ext_ref[start + 5 : start + 5 + length, lanes]
    for k in range(1, CONV):
        summed = summed + taps_ref[k : k + 1, lanes] * ext_ref[start + 5 + k : start + 5 + k + length, lanes]
    return summed


def conv_back(grad_ref, taps_ref, start, length, lanes):
    raw = taps_ref[CONV - 1 : CONV, lanes] * grad_ref[start : start + length, lanes]
    for j in range(1, CONV):
        raw = raw + taps_ref[CONV - 1 - j : CONV - j, lanes] * grad_ref[start + j : start + j + length, lanes]
    return raw


def as_column(row):
    return jnp.broadcast_to(row, (LANES, LANES)).T


def row_sums(value):
    ones = jnp.ones((8, LANES), BF16)
    parts = thirds(value)
    return mm(ones, parts[0], 1, 1) + (mm(ones, parts[1], 1, 1) + mm(ones, parts[2], 1, 1))


def triangle(length, lower):
    row = lax.broadcasted_iota(jnp.int32, (length, length), 0)
    column = lax.broadcasted_iota(jnp.int32, (length, length), 1)
    return row >= column if lower else row <= column


ANYWHERE = pl.BlockSpec(memory_space=pl.ANY)


class Order:
    def __init__(self):
        self.now, self.pending, self.shape = None, [], (8, 2048)

    def before_next(self, *arrays):
        self.pending += [array for array in arrays if array.dtype != F16]

    def fence(self):
        tokens = self.pending + ([] if self.now is None else [self.now])
        self.pending = []

        def body(*refs):
            refs[-1][...] = jnp.zeros_like(refs[-1])

        self.now = pl.pallas_call(
            body,
            in_specs=[ANYWHERE] * len(tokens),
            out_shape=SHAPE(self.shape, F32),
            compiler_params=pltpu.CompilerParams(vmem_limit_bytes=VMEM_LIMIT),
            name="fence",
        )(*tokens)

    def tie(self, value):
        if self.now is None:
            return value
        zeros = lax.slice(self.now, (0, 0), (1, value.shape[-1])).astype(value.dtype)
        return value + zeros.reshape((1,) * (value.ndim - 1) + (value.shape[-1],))

    def call(self, kernel, operands, *, meta, grid, in_specs, out_specs, out_shape, scratch=(), flops, moved, name, aliases=None):
        tokens = self.pending + ([] if self.now is None else [self.now])
        inputs, outputs = len(operands), len(out_shape)
        self.pending = []

        def body(meta_ref, *refs):
            last = inputs + len(tokens) + outputs
            refs[last][...] = jnp.zeros_like(refs[last])
            kernel(meta_ref, *refs[:inputs], *refs[inputs + len(tokens) : last], *refs[last + 1 :])

        result = pl.pallas_call(
            body,
            grid_spec=pltpu.PrefetchScalarGridSpec(
                num_scalar_prefetch=1,
                grid=grid,
                in_specs=list(in_specs) + [ANYWHERE] * len(tokens),
                out_specs=list(out_specs) + [whole(self.shape)],
                scratch_shapes=list(scratch),
            ),
            out_shape=list(out_shape) + [SHAPE(self.shape, F32)],
            input_output_aliases=aliases or {},
            compiler_params=pltpu.CompilerParams(
                vmem_limit_bytes=VMEM_LIMIT, dimension_semantics=("arbitrary",) * len(grid)
            ),
            cost_estimate=pl.CostEstimate(flops=int(flops), bytes_accessed=int(moved), transcendentals=0),
            name=name,
        )(meta, *operands, *tokens)
        self.now = result[-1]
        return result[:-1]


def constants_kernel(lengths_ref, step_bias_ref, decay_ref, skip_ref, out_gain_ref, meta_ref, head_ref, chan_ref, expand_ref, *, slots):
    seqs, heads = lengths_ref.shape[0], step_bias_ref.shape[1]
    channels = out_gain_ref.shape[1]
    place, least = jnp.int32(0), lengths_ref[0]
    for s in range(1, seqs):
        shorter = lengths_ref[s] < least
        place, least = jnp.where(shorter, s, place), jnp.where(shorter, lengths_ref[s], least)
    first = lax.axis_index("seq") * slots
    for s in range(seqs):
        source = jnp.where(place == s, seqs - 1, s) if s < seqs - 1 else place
        meta_ref[s] = source
        meta_ref[seqs + s] = lengths_ref[source] - first
    mine, count = lax.axis_index("head"), lax.axis_size("head")
    meta_ref[2 * seqs] = jnp.where((mine == 0) | (mine == count - 1), 1, 0)
    lane = lax.broadcasted_iota(jnp.int32, (8, LANES), 1)
    row = lax.broadcasted_iota(jnp.int32, (8, LANES), 0)
    pad = lambda ref: jnp.concatenate([ref[...], jnp.zeros((1, LANES - heads), F32)], axis=1)
    head_ref[...] = jnp.zeros((8, LANES), F32)
    head_ref[0:1, :] = pad(step_bias_ref)
    head_ref[1:2, :] = pad(decay_ref)
    chan_ref[...] = jnp.zeros_like(chan_ref)
    chan_ref[0:1, :] = spread(rows8(pad(skip_ref)), channels)[0:1, :]
    chan_ref[1:2, :] = out_gain_ref[...]
    head_of = lax.broadcasted_iota(jnp.int32, (LANES, channels), 1) // HEAD_DIM
    expand_ref[...] = jnp.where(head_of == lax.broadcasted_iota(jnp.int32, (LANES, channels), 0), 1.0, 0.0).astype(BF16)


def normalized(rows, gain):
    u = rows.astype(F32)
    scale = lax.rsqrt(jnp.mean(u * u, axis=-1, keepdims=True) + EPSILON)
    return (u * scale * gain).astype(BF16)


def project_kernel(
    meta_ref, u_ref, cot_ref, gain_ref, gate_ref, x_ref, step_ref, out_ref, normed_ref, branch_ref, proj_ref, gh_ref,
    peak_ref, *, first
):
    @pl.when((pl.program_id(1) == 0) & (pl.program_id(0) == 0))
    def _():
        peak_ref[...] = jnp.zeros_like(peak_ref)

    rows, channels = u_ref.shape[0], gate_ref.shape[1]
    normed = normalized(u_ref[...], gain_ref[...])
    normed_ref[...] = normed
    at = pl.program_id(1) * rows + lax.broadcasted_iota(jnp.int32, cot_ref.shape, 0)
    live = at < meta_ref[4 + first + pl.program_id(0)]
    branch = jnp.where(live, cot_ref[...].astype(F32), 0.0)
    peak_ref[...] = jnp.maximum(peak_ref[...], peak8(branch))
    branch = branch.astype(BF16)
    branch_ref[...] = branch
    proj_ref[:, :channels] = mm(normed, gate_ref[...])
    proj_ref[:, channels : 2 * channels] = mm(normed, x_ref[...])
    proj_ref[:, 2 * channels :] = mm(normed, step_ref[...])
    gh_ref[...] = mm(branch, out_ref[...], 1, 1)


def edge_kernel(meta_ref, before_ref, gain_ref, x_ref, pair_ref, xhalo_ref, bchalo_ref):
    seqs, rows, width = before_ref.shape
    normed = normalized(before_ref[...].reshape(seqs * rows, width), gain_ref[...])
    xhalo_ref[...] = mm(normed, x_ref[...]).reshape(xhalo_ref.shape)
    bchalo_ref[...] = mm(normed, pair_ref[...]).reshape(bchalo_ref.shape)


def local_state_kernel(
    meta_ref, x_ref, xhalo_ref, normed_ref, pair_ref, bchalo_ref, step_ref, taps_ref, bias_ref, btaps_ref, bbias_ref,
    head_ref, xs_ref, raw_ref, bcs_ref, sc_ref, end_ref, xe, be, state, total,
):
    c, rows = pl.program_id(1), x_ref.shape[0]
    channels = x_ref.shape[1]

    @pl.when(c == 0)
    def _():
        xe[0:8, :] = xhalo_ref[...]
        be[0:8, :] = bchalo_ref[...]
        state[...] = jnp.zeros_like(state)
        total[...] = jnp.zeros_like(total)

    xe[8 : 8 + rows, :] = x_ref[...]
    raw = mm(normed_ref[...], pair_ref[...])
    raw_ref[...] = raw
    be[8 : 8 + rows, :] = raw
    lower = triangle(CHUNK, True).astype(BF16)
    left = left_half(CHUNK)
    lane = lax.broadcasted_iota(I32, (CHUNK, LANES), 1)
    for at in range(0, rows, CHUNK):
        here = slice(at, at + CHUNK)
        for lanes in (slice(0, STATE), slice(STATE, 2 * STATE)):
            pb = conv(be, btaps_ref, bbias_ref, at, CHUNK, lanes)
            bcs_ref[here, lanes] = pb * sigmoid(pb)
        step = softplus(step_ref[here, :] + head_ref[0:1, :])
        cum = summed_by(lower, -step * jnp.exp(head_ref[1:2, :]))
        sc_ref[here, :] = jnp.where(lane < HALF, step, pltpu.roll(cum, HALF, 1))
        end = cum[CHUNK - 1 : CHUNK, :]
        fading = step * jnp.exp(end - cum)
        keep = spread(rows8(jnp.exp(end)), channels)
        bt2 = halves(bcs_ref[here, :STATE].T)
        for pair in range(channels // LANES):
            lanes = slice(pair * LANES, (pair + 1) * LANES)
            p = conv(xe, taps_ref, bias_ref, at, CHUNK, lanes)
            xs = p * sigmoid(p)
            xs_ref[here, lanes] = xs
            weighted = halves(xs * spread_pair(fading, pair, left))
            state[:, lanes] = keep[0:1, lanes] * state[:, lanes] + dot3(bt2, weighted)
        total[...] += rows8(end)
    xe[0:8, :] = xe[rows : rows + 8, :]
    be[0:8, :] = be[rows : rows + 8, :]

    @pl.when(c == pl.num_programs(1) - 1)
    def _():
        end_ref[0:STATE, :] = state[...]
        end_ref[STATE : STATE + 8, :] = spread(jnp.exp(total[...]), channels)


def mix_kernel(
    meta_ref, xs_ref, bcs_ref, sc_ref, start_ref, gate_ref, gh_ref, chan_ref,
    mixed_ref, red_ref, states_ref, final_ref, state,
):
    c, rows = pl.program_id(1), xs_ref.shape[0]
    channels = xs_ref.shape[1]

    @pl.when(c == 0)
    def _():
        state[...] = start_ref[...]

    lower = triangle(CHUNK, True)
    left = left_half(CHUNK)
    zero = jnp.zeros((CHUNK, LANES), BF16)
    for at in range(0, rows, CHUNK):
        here = slice(at, at + CHUNK)
        entering = state[...]
        states_ref[at // CHUNK] = entering
        sc = sc_ref[here, :]
        sc_t = sc.T
        b2, c2 = halves(bcs_ref[here, :STATE]), halves(bcs_ref[here, STATE:])
        bt2 = halves(bcs_ref[here, :STATE].T)
        scores = dot3_t(c2, b2)
        carried = dot3(c2, halves(entering))
        end_full = spread(rows8(pltpu.roll(sc, HALF, 1)[CHUNK - 1 : CHUNK, :]), channels)
        sq = jnp.zeros((CHUNK, LANES), F32)
        dt = jnp.zeros((CHUNK, LANES), F32)
        for pair in range(channels // LANES):
            lanes = slice(pair * LANES, (pair + 1) * LANES)
            xs = xs_ref[here, lanes]
            weighted = xs * spread_pair(sc, pair, left)
            high, low = halves(weighted)
            stacked, columns = [], []
            for h in (HALF + 2 * pair, HALF + 2 * pair + 1):
                column = jnp.broadcast_to(sc[:, h : h + 1], (CHUNK, LANES))
                columns.append(column)
                mixing = jnp.where(lower, jnp.exp(column - sc_t[h : h + 1, :]), 0.0) * scores
                stacked.append(jnp.concatenate(halves(mixing), axis=1))
            right = jnp.concatenate(
                [jnp.concatenate([high, low], axis=1), jnp.concatenate([high, zero], axis=1)], axis=0
            )
            out = mm(jnp.concatenate(stacked, axis=0), right)
            out = out[:, :LANES] + out[:, LANES:]
            cum_full = jnp.where(left, columns[0], columns[1])
            mixed = (
                jnp.where(left, out[:CHUNK], out[CHUNK:])
                + carried[:, lanes] * jnp.exp(cum_full)
                + chan_ref[0:1, lanes] * xs
            )
            mixed_ref[here, lanes] = mixed
            gate = gate_ref[here, lanes]
            gated = mixed * (gate * sigmoid(gate))
            sq = sq + gated * gated
            dt = dt + gated * (gh_ref[here, lanes] * chan_ref[1:2, lanes])
            tail = end_full[0:1, lanes]
            later = halves(weighted * jnp.exp(tail - cum_full))
            state[:, lanes] = jnp.exp(tail) * state[:, lanes] + dot3(bt2, later)
        row = lax.broadcasted_iota(I32, (8, CHUNK), 0)
        red_ref[:, here] = jnp.where(row == 0, row_sums(sq), row_sums(dt))

    @pl.when(c == pl.num_programs(1) - 1)
    def _():
        final_ref[...] = state[...]


def gate_back_kernel(
    meta_ref, mixed_ref, gate_ref, gh_ref, row_ref, bcs_ref, sc_ref, chan_ref,
    hidden_ref, ggate_ref, dy_ref, gend_ref, acc_ref, grad, total,
):
    c, rows = pl.program_id(1), mixed_ref.shape[0]
    channels = mixed_ref.shape[1]

    @pl.when(c == 0)
    def _():
        grad[...] = jnp.zeros_like(grad)
        total[...] = jnp.zeros_like(total)

    @pl.when((c == 0) & (pl.program_id(0) == 0))
    def _():
        acc_ref[...] = jnp.zeros_like(acc_ref)

    left = left_half(CHUNK)
    for at in reversed(range(0, rows, CHUNK)):
        here = slice(at, at + CHUNK)
        cum = pltpu.roll(sc_ref[here, :], HALF, 1)
        ct2 = halves(bcs_ref[here, STATE:].T)
        keep = spread(rows8(jnp.exp(cum[CHUNK - 1 : CHUNK, :])), channels)
        grown = jnp.exp(cum)
        squares, dots = as_column(row_ref[0:1, here]), as_column(row_ref[1:2, here])
        r = lax.rsqrt(squares * (1.0 / INNER) + EPSILON)
        pull = r * r * r * dots * (1.0 / INNER)
        for pair in range(channels // LANES):
            lanes = slice(pair * LANES, (pair + 1) * LANES)
            mixed, gate, gh = mixed_ref[here, lanes], gate_ref[here, lanes], gh_ref[here, lanes]
            out_gain = chan_ref[1:2, lanes]
            sig = sigmoid(gate)
            silu = gate * sig
            gated = mixed * silu
            normal = gated * r
            hidden_ref[here, lanes] = (normal * out_gain).astype(BF16)
            acc_ref[:, lanes] += fold8(gh * normal)
            grad_gated = r * (gh * out_gain) - gated * pull
            dy = grad_gated * silu
            dy_ref[here, lanes] = dy
            ggate_ref[here, lanes] = (grad_gated * mixed * (sig * (1.0 + gate * (1.0 - sig)))).astype(BF16)
            grad[:, lanes] = keep[0:1, lanes] * grad[:, lanes] + dot3(
                ct2, halves(dy * spread_pair(grown, pair, left))
            )
        total[...] += rows8(cum[CHUNK - 1 : CHUNK, :])

    @pl.when(c == pl.num_programs(1) - 1)
    def _():
        gend_ref[0:STATE, :] = grad[...]
        gend_ref[STATE : STATE + 8, :] = spread(jnp.exp(total[...]), channels)


def state_back_kernel(
    meta_ref, x_ref, xprev_ref, xhalo_ref, bcs_ref, sc_ref, step_ref, dy_ref, mixed_ref, states_ref, final_ref,
    gin_ref, ggate_ref, taps_ref, bias_ref, head_ref, chan_ref, expand_ref, *refs
):
    gp_ref, dbc_ref, tail_ref, first_ref, acc_ref, hacc_ref = refs[-15:-9]
    xe, ge, grad, flux, wide, wlow, dhigh, dlow, sums = refs[-9:]
    c, rows = pl.program_id(1), x_ref.shape[0]
    blocks = pl.num_programs(1)
    channels = x_ref.shape[1]
    expand = expand_ref[...]

    @pl.when((c == 0) & (pl.program_id(0) == 0))
    def _():
        acc_ref[...] = jnp.zeros_like(acc_ref)
        hacc_ref[...] = jnp.zeros_like(hacc_ref)

    @pl.when(c == 0)
    def _():
        grad[...] = gin_ref[...]
        ending = per_head(fold8(grad[...] * final_ref[...]), expand)
        flux[...] = rows8(jnp.sum(ending, axis=0, keepdims=True))
        ge[rows : rows + 8, :] = jnp.zeros((8, channels), F32)

    @pl.when(c != 0)
    def _():
        ge[rows : rows + 8, :] = ge[0:8, :]

    @pl.when(c == blocks - 1)
    def _():
        xe[0:8, :] = xhalo_ref[...]

    @pl.when(c != blocks - 1)
    def _():
        xe[0:8, :] = xprev_ref[...]

    xe[8 : 8 + rows, :] = x_ref[...]
    gp_ref[:, :channels] = ggate_ref[...]
    upper = triangle(CHUNK, False)
    left = left_half(CHUNK)
    zero = jnp.zeros((CHUNK, LANES), BF16)
    turn = lambda value: pltpu.roll(value.astype(F32), HEAD_DIM, 1).astype(BF16)
    for at in reversed(range(0, rows, CHUNK)):
        here = slice(at, at + CHUNK)
        sc = sc_ref[here, :]
        sc_t = sc.T
        cum = pltpu.roll(sc, HALF, 1)
        end_full = spread(rows8(cum[CHUNK - 1 : CHUNK, :]), channels)
        b2, c2 = halves(bcs_ref[here, :STATE]), halves(bcs_ref[here, STATE:])
        ct2 = halves(bcs_ref[here, STATE:].T)
        scores_t = dot3_t(b2, c2)
        leaving2 = halves(grad[...])
        pulled = dot3(b2, leaving2)
        dscores_t = jnp.zeros((CHUNK, CHUNK), F32)
        for pair in range(channels // LANES):
            lanes = slice(pair * LANES, (pair + 1) * LANES)
            p = conv(xe, taps_ref, bias_ref, at, CHUNK, lanes)
            sig = sigmoid(p)
            xs = p * sig
            slope = sig * (1.0 + p * (1.0 - sig))
            step_full = spread_pair(sc, pair, left)
            weighted = xs * step_full
            wh, wl = halves(weighted)
            dy = dy_ref[here, lanes]
            dh, dl = halves(dy)
            turned_wh, turned_wl, turned_dh = turn(wh), turn(wl), turn(dh)
            w_rows = (
                jnp.concatenate([jnp.where(left, wh, turned_wl), jnp.where(left, wh, zero)], axis=1),
                jnp.concatenate([jnp.where(left, turned_wh, wl), jnp.where(left, zero, wh)], axis=1),
            )
            d_rows = (
                jnp.concatenate([jnp.where(left, dh, turned_dh), dl], axis=1),
                jnp.concatenate([jnp.where(left, turned_dh, dh), dl], axis=1),
            )
            stacked, columns = [], []
            for side, h in enumerate((HALF + 2 * pair, HALF + 2 * pair + 1)):
                column = jnp.broadcast_to(sc[:, h : h + 1], (CHUNK, LANES))
                columns.append(column)
                kern = jnp.where(upper, jnp.exp(sc_t[h : h + 1, :] - column), 0.0)
                dscores_t = dscores_t + kern * mm(w_rows[side], d_rows[side], 1, 1)
                stacked.append(jnp.concatenate(halves(kern * scores_t), axis=1))
            right = jnp.concatenate(
                [jnp.concatenate([dh, dl], axis=1), jnp.concatenate([dh, zero], axis=1)], axis=0
            )
            out = mm(jnp.concatenate(stacked, axis=0), right)
            out = out[:, :LANES] + out[:, LANES:]
            cum_full = jnp.where(left, columns[0], columns[1])
            fade = jnp.exp(end_full[0:1, lanes] - cum_full)
            dxw = jnp.where(left, out[:CHUNK], out[CHUNK:]) + pulled[:, lanes] * fade
            grad_xs = step_full * dxw + chan_ref[0:1, lanes] * dy
            wide[:, lanes], wlow[:, lanes] = halves(weighted * fade)
            gh, gl = halves(dy * jnp.exp(cum_full))
            dhigh[:, lanes], dlow[:, lanes] = gh, gl
            keep = jnp.exp(end_full[0:1, lanes])
            grad[:, lanes] = keep * grad[:, lanes] + dot3(ct2, (gh, gl))
            sums[0:CHUNK, lanes] = xs * dxw
            sums[CHUNK:, lanes] = dy * mixed_ref[here, lanes] - xs * grad_xs
            grad_p = grad_xs * slope
            ge[here, lanes] = grad_p
            for k in range(CONV):
                acc_ref[8 * k : 8 * k + 8, lanes] += fold8(grad_p * xe[at + 5 + k : at + 5 + k + CHUNK, lanes])
            acc_ref[32:40, lanes] += fold8(grad_p)
            acc_ref[40:48, lanes] += fold8(dy * xs)
            raw = conv_back(ge, taps_ref, at, CHUNK, lanes)
            gp_ref[here, channels + pair * LANES : channels + (pair + 1) * LANES] = raw.astype(BF16)
            if at == rows - CHUNK:
                tail_ref[:, lanes] = raw[CHUNK - 8 :, :]
        entering2 = halves(states_ref[at // CHUNK])
        dscores2 = halves(dscores_t)
        dscores_back = halves(dscores_t.T)
        dbc_ref[here, :STATE] = dot3(dscores2, c2) + dot3_t((wide[...], wlow[...]), leaving2)
        dbc_ref[here, STATE:] = dot3(dscores_back, b2) + dot3_t((dhigh[...], dlow[...]), entering2)
        both = per_head(sums[...], expand)
        grad_rate = summed_by(upper.astype(BF16), both[CHUNK:]) + flux[0:1, :]
        flux[...] = rows8(grad_rate[0:1, :])
        rate_of = jnp.exp(head_ref[1:2, :])
        grad_step = both[:CHUNK] - rate_of * grad_rate
        grad_raw = grad_step * sigmoid(step_ref[here, :] + head_ref[0:1, :])
        hacc_ref[0:8, :] += fold8(grad_raw)
        hacc_ref[8:16, :] += fold8(-rate_of * jnp.where(lax.broadcasted_iota(I32, sc.shape, 1) < HALF, sc, 0.0) * grad_rate)
        gp_ref[here, 2 * channels :] = grad_raw.astype(BF16)

    @pl.when(c == blocks - 1)
    def _():
        first_ref[...] = ge[0:8, :]


def pair_back_kernel(
    meta_ref, raw_ref, halo_ref, g_ref, taps_ref, bias_ref, out_ref, tail_ref, first_ref, acc_ref, xe, ge
):
    length, channels = raw_ref.shape

    @pl.when(pl.program_id(0) == 0)
    def _():
        acc_ref[...] = jnp.zeros_like(acc_ref)

    xe[0:8, :] = halo_ref[...]
    xe[8 : 8 + length, :] = raw_ref[...]
    ge[length : length + 8, :] = jnp.zeros((8, channels), F32)
    for at in range(0, length, CHUNK):
        here = slice(at, at + CHUNK)
        for half in range(2):
            lanes = slice(half * STATE, (half + 1) * STATE)
            p = conv(xe, taps_ref, bias_ref, at, CHUNK, lanes)
            sig = sigmoid(p)
            grad_p = g_ref[here, lanes] * (sig * (1.0 + p * (1.0 - sig)))
            ge[here, lanes] = grad_p
            for k in range(CONV):
                acc_ref[8 * k : 8 * k + 8, lanes] += fold8(grad_p * xe[at + 5 + k : at + 5 + k + CHUNK, lanes])
            acc_ref[32:40, lanes] += fold8(grad_p)
    for at in range(0, length, CHUNK):
        for lanes in (slice(0, STATE), slice(STATE, 2 * STATE)):
            raw = conv_back(ge, taps_ref, at, CHUNK, lanes)
            out_ref[at : at + CHUNK, lanes] = raw.astype(BF16)
            if at == length - CHUNK:
                tail_ref[:, lanes] = raw[CHUNK - 8 :, :]
    first_ref[...] = ge[0:8, :]


def finish_kernel(meta_ref, gn_ref, u_ref, branch_ref, gbc_ref, weight_ref, gain_ref, *refs):
    out_ref, acc_ref = refs[-2:]

    @pl.when((pl.program_id(1) == 0) & (pl.program_id(0) == 0))
    def _():
        acc_ref[...] = jnp.zeros_like(acc_ref)

    u = u_ref[...].astype(F32)
    scale = lax.rsqrt(jnp.mean(u * u, axis=-1, keepdims=True) + EPSILON)
    grad = gn_ref[...] + mm(gbc_ref[...], weight_ref[...], 1, 1)
    normal = u * scale
    acc_ref[...] += fold8(grad * normal)
    w = grad * gain_ref[...]
    pull = scale * jnp.mean(w * normal, axis=-1, keepdims=True)
    out_ref[...] = scale * w - normal * pull + branch_ref[...].astype(F32)


def place_kernel(meta_ref, own_ref, got_ref, *refs, takes_at):
    out_ref = refs[-1]
    takes = meta_ref[takes_at] == 1

    @pl.when(takes)
    def _():
        out_ref[...] = got_ref[...]

    @pl.when(jnp.logical_not(takes))
    def _():
        out_ref[...] = own_ref[...]


SHAPE = jax.ShapeDtypeStruct


def whole(shape):
    return pl.BlockSpec(shape, lambda s, c, meta: (0,) * len(shape))


def per_seq(rows, width):
    return pl.BlockSpec((None, rows, width), lambda s, c, meta: (s, 0, 0))


def forward_rows(width, column):
    return pl.BlockSpec((None, ROWS, width), lambda s, c, meta: (s, c, column))


def constants(lengths, step_bias, decay_log, skip_gain, out_gain, slots):
    seqs, channels = lengths.shape[0], out_gain.shape[0]
    row = lambda value: value[None]
    smem = pl.BlockSpec(memory_space=pltpu.SMEM)
    vmem = pl.BlockSpec(memory_space=pltpu.VMEM)
    return pl.pallas_call(
        functools.partial(constants_kernel, slots=slots),
        in_specs=[smem] + [vmem] * 4,
        out_specs=[smem, vmem, vmem, vmem],
        out_shape=[
            SHAPE((2 * seqs + 1,), jnp.int32), SHAPE((8, LANES), F32), SHAPE((8, channels), F32),
            SHAPE((LANES, channels), BF16),
        ],
        name="constants",
    )(lengths, row(step_bias), row(decay_log), row(skip_gain), row(out_gain))


def project(order, meta, residual_in, cotangent, gain, gate, x, step, out, first, count):
    seqs, slots, width = residual_in.shape
    channels = gate.shape[1]
    rows = 256
    placed = pl.BlockSpec((None, rows, width), lambda s, c, meta: (meta[s + first], c, 0))
    plain = lambda wide: pl.BlockSpec((None, rows, wide), lambda s, c, meta: (s, c, 0))
    wide = 2 * channels + LANES
    return order.call(
        functools.partial(project_kernel, first=first),
        (residual_in, cotangent, gain, gate, x, step, out),
        meta=meta,
        grid=(count, slots // rows),
        in_specs=[placed, placed] + [whole(a.shape) for a in (gain, gate, x, step, out)],
        out_specs=[plain(width), plain(width), plain(wide), plain(channels), whole((8, width))],
        out_shape=[
            SHAPE((count, slots, width), BF16), SHAPE((count, slots, width), BF16),
            SHAPE((count, slots, wide), F32), SHAPE((count, slots, channels), F32), SHAPE((8, width), F32),
        ],
        flops=2 * count * slots * width * (wide + channels),
        moved=count * slots * (width * 8 + wide * 4),
        name="project",
    )


def edge_halos(order, meta, before, gain, x, pair):
    seqs = before.shape[0]
    operands = (before, gain, x, pair)
    shapes = [(seqs, 8, x.shape[1]), (seqs, 8, pair.shape[1])]
    return order.call(
        edge_kernel,
        operands,
        meta=meta,
        grid=(1, 1),
        in_specs=[whole(a.shape) for a in operands],
        out_specs=[whole(a) for a in shapes],
        out_shape=[SHAPE(a, F32) for a in shapes],
        flops=1e8,
        moved=4e6,
        name="edge_halos",
    )


def local_states(order, meta, proj, normed, pair, halo_x, halo_bc, taps, bias, btaps, bbias, head, first, channels):
    count, slots, _ = proj.shape
    placed = lambda width: pl.BlockSpec((None, 8, width), lambda s, c, meta: (meta[first + s], 0, 0))
    return order.call(
        local_state_kernel,
        (proj, halo_x, normed, pair, halo_bc, proj, taps, bias, btaps, bbias, head),
        meta=meta,
        grid=(count, slots // ROWS),
        in_specs=[
            forward_rows(channels, 1), placed(channels), forward_rows(normed.shape[2], 0), whole(pair.shape),
            placed(2 * STATE),
            forward_rows(LANES, 2 * channels // LANES), whole(taps.shape), whole(bias.shape), whole(btaps.shape),
            whole(bbias.shape), whole(head.shape),
        ],
        out_specs=[
            forward_rows(channels, 0), forward_rows(2 * STATE, 0), forward_rows(2 * STATE, 0),
            forward_rows(LANES, 0), per_seq(STATE + 8, channels),
        ],
        out_shape=[
            SHAPE((count, slots, channels), F32), SHAPE((count, slots, 2 * STATE), F32),
            SHAPE((count, slots, 2 * STATE), F32),
            SHAPE((count, slots, LANES), F32), SHAPE((count, STATE + 8, channels), F32),
        ],
        scratch=[
            pltpu.VMEM((ROWS + 8, channels), F32), pltpu.VMEM((ROWS + 8, 2 * STATE), F32),
            pltpu.VMEM((STATE, channels), F32), pltpu.VMEM((8, LANES), F32),
        ],
        flops=count * 4e9,
        moved=count * slots * channels * 8,
        name="local_states",
    )


def mix(order, meta, xs, bcs, sc, start, proj, grad_hidden, chan):
    count, slots, channels = xs.shape
    chunks = slots // CHUNK
    return order.call(
        mix_kernel,
        (xs, bcs, sc, start, proj, grad_hidden, chan),
        meta=meta,
        grid=(count, slots // ROWS),
        in_specs=[
            forward_rows(channels, 0), forward_rows(2 * STATE, 0), forward_rows(LANES, 0),
            per_seq(STATE, channels),
            forward_rows(channels, 0), forward_rows(channels, 0), whole(chan.shape),
        ],
        out_specs=[
            forward_rows(channels, 0), pl.BlockSpec((None, 8, ROWS), lambda s, c, meta: (s, 0, c)),
            pl.BlockSpec((None, ROWS // CHUNK, STATE, channels), lambda s, c, meta: (s, c, 0, 0)),
            per_seq(STATE, channels),
        ],
        out_shape=[
            SHAPE((count, slots, channels), F32), SHAPE((count, 8, slots), F32),
            SHAPE((count, chunks, STATE, channels), F32), SHAPE((count, STATE, channels), F32),
        ],
        scratch=[pltpu.VMEM((STATE, channels), F32)],
        flops=count * 6e9,
        moved=count * slots * channels * 20,
        name="mix",
    )


def gate_back(order, meta, mixed, proj, grad_hidden, rows, bcs, sc, chan):
    count, slots, channels = mixed.shape
    chunks = slots // ROWS
    row = lambda width, column: pl.BlockSpec(
        (None, ROWS, width), lambda s, c, meta: (s, chunks - 1 - c, column)
    )
    return order.call(
        gate_back_kernel,
        (mixed, proj, grad_hidden, rows, bcs, sc, chan),
        meta=meta,
        grid=(count, chunks),
        in_specs=[
            row(channels, 0), row(channels, 0), row(channels, 0),
            pl.BlockSpec((None, 8, ROWS), lambda s, c, meta: (s, 0, chunks - 1 - c)), row(2 * STATE, 0),
            row(LANES, 0), whole(chan.shape),
        ],
        out_specs=[
            row(channels, 0), row(channels, 0), row(channels, 0), per_seq(STATE + 8, channels),
            whole((8, channels)),
        ],
        out_shape=[
            SHAPE((count, slots, channels), BF16), SHAPE((count, slots, channels), BF16),
            SHAPE((count, slots, channels), F32), SHAPE((count, STATE + 8, channels), F32),
            SHAPE((8, channels), F32),
        ],
        scratch=[pltpu.VMEM((STATE, channels), F32), pltpu.VMEM((8, LANES), F32)],
        flops=count * 4e9,
        moved=count * slots * channels * 20,
        name="gate_back",
    )


def state_back(
    order, meta, at, first, proj, halo_x, bcs, sc, dy, mixed, states, final, grad_in, grad_gate, taps, bias, head, chan, expand,
    earlier,
):
    count, slots, channels = mixed.shape
    chunks = slots // ROWS
    tiles = ROWS // 8
    row = lambda width, column, s=at: pl.BlockSpec(
        (None, ROWS, width), lambda _, c, meta: (s, chunks - 1 - c, column)
    )
    only = lambda rows, width, s=at: pl.BlockSpec((None, rows, width), lambda _, c, meta: (s, 0, 0))
    before = pl.BlockSpec(
        (None, 8, channels), lambda _, c, meta: (at, jnp.maximum((chunks - 1 - c) * tiles - 1, 0), 1)
    )
    tail = pl.BlockSpec((None, None, 8, channels), lambda _, c, meta: (at, chunks - 1 - c, 0, 0))
    extra = () if earlier is None else tuple(earlier)
    return order.call(
        state_back_kernel,
        (
            proj, proj, halo_x, bcs, sc, proj, dy, mixed, states, final, grad_in, grad_gate, taps, bias, head, chan,
            expand,
        ) + extra,
        meta=meta,
        grid=(1, chunks),
        in_specs=[
            row(channels, 1), before,
            pl.BlockSpec((None, 8, channels), lambda _, c, meta: (meta[first + at], 0, 0)),
            row(2 * STATE, 0), row(LANES, 0),
            row(LANES, 2 * channels // LANES), row(channels, 0), row(channels, 0),
            pl.BlockSpec((None, ROWS // CHUNK, STATE, channels), lambda _, c, meta: (at, chunks - 1 - c, 0, 0)),
            only(STATE, channels),
            only(STATE, channels),
            row(channels, 0),
            whole(taps.shape), whole(bias.shape), whole(head.shape), whole(chan.shape), whole(expand.shape),
        ] + [ANYWHERE] * len(extra),
        out_specs=[
            row(2 * channels + LANES, 0), row(2 * STATE, 0), tail, only(8, channels),
            whole((48, channels)), whole((16, LANES)),
        ],
        out_shape=[
            SHAPE((count, slots, 2 * channels + LANES), BF16), SHAPE((count, slots, 2 * STATE), F32),
            SHAPE((count, chunks, 8, channels), F32), SHAPE((count, 8, channels), F32),
            SHAPE((48, channels), F32), SHAPE((16, LANES), F32),
        ],
        scratch=[
            pltpu.VMEM((ROWS + 8, channels), F32), pltpu.VMEM((ROWS + 8, channels), F32),
            pltpu.VMEM((STATE, channels), F32), pltpu.VMEM((8, LANES), F32),
            pltpu.VMEM((CHUNK, channels), BF16), pltpu.VMEM((CHUNK, channels), BF16),
            pltpu.VMEM((CHUNK, channels), BF16), pltpu.VMEM((CHUNK, channels), BF16),
            pltpu.VMEM((2 * CHUNK, channels), F32),
        ],
        aliases={18 + i: i for i in range(4)} if extra else None,
        flops=12e9,
        moved=slots * channels * 24,
        name="state_back",
    )


def pair_back(order, meta, first, raw, halo, grad, taps, bias):
    count, slots, channels = raw.shape
    placed = pl.BlockSpec((None, 8, channels), lambda s, c, meta: (meta[first + s], 0, 0))
    return order.call(
        pair_back_kernel,
        (raw, halo, grad, taps, bias),
        meta=meta,
        grid=(count, 1),
        in_specs=[
            per_seq(slots, channels), placed, per_seq(slots, channels), whole(taps.shape), whole(bias.shape),
        ],
        out_specs=[
            per_seq(slots, channels), per_seq(8, channels), per_seq(8, channels), whole((40, channels)),
        ],
        out_shape=[
            SHAPE((count, slots, channels), BF16), SHAPE((count, 8, channels), F32),
            SHAPE((count, 8, channels), F32), SHAPE((40, channels), F32),
        ],
        scratch=[pltpu.VMEM((slots + 8, channels), F32), pltpu.VMEM((slots + 8, channels), F32)],
        flops=count * 1e9,
        moved=count * slots * channels * 10,
        name="pair_back",
    )


def finish(order, meta, grad_normed, residual_in, branch, gbc, weight, gain, at, local, target):
    seqs, slots, width = residual_in.shape
    rows = 256
    placed = pl.BlockSpec((None, rows, width), lambda s, c, meta: (meta[at], c, 0))
    fixed = lambda where, wide: pl.BlockSpec((None, rows, wide), lambda s, c, meta: (where, c, 0))
    extra = () if target is None else (target,)
    return order.call(
        finish_kernel,
        (grad_normed, residual_in, branch, gbc, weight, gain) + extra,
        meta=meta,
        grid=(1, slots // rows),
        in_specs=[
            fixed(0, width), placed, fixed(local, width), fixed(local, gbc.shape[2]),
            whole(weight.shape), whole(gain.shape),
        ] + [ANYWHERE] * len(extra),
        out_specs=[placed, whole((8, width))],
        out_shape=[SHAPE((seqs, slots, width), F32), SHAPE((8, width), F32)],
        aliases={7: 0} if extra else None,
        flops=1e9,
        moved=slots * width * 14,
        name="finish",
    )


def place(order, meta, own, got, at, seqs, target):
    count, slots, width = own.shape
    rows = 256
    plain = pl.BlockSpec((None, rows, width), lambda s, c, meta: (s, c, 0))
    placed = pl.BlockSpec((None, rows, width), lambda s, c, meta: (meta[at + s], c, 0))
    extra = () if target is None else (target,)
    return order.call(
        functools.partial(place_kernel, takes_at=2 * seqs),
        (own, got) + extra,
        meta=meta,
        grid=(count, slots // rows),
        in_specs=[plain, plain] + [ANYWHERE] * len(extra),
        out_specs=[placed],
        out_shape=[SHAPE((seqs, slots, width), own.dtype)],
        aliases={3: 0} if extra else None,
        flops=1e6,
        moved=count * slots * width * 6,
        name="place",
    )[0]


class Running:
    def __init__(self, order, steps):
        self.order, self.steps, self.value, self.ended = order, steps, None, False
        self.advance()

    def advance(self, times=1):
        for _ in range(times):
            if self.ended:
                return self
            try:
                self.sent = next(self.steps)
                self.order.before_next(*self.sent)
            except StopIteration as stop:
                self.value, self.ended = stop.value, True
        return self

    def pin(self):
        self.order.before_next(*(array[:8, :LANES].astype(F32) for array in self.sent))
        return self

    def end(self):
        while not self.ended:
            self.advance()
        return self.value


def line_sum(order, part, axis, finish, choose=True):
    count, mine = lax.axis_size(axis), lax.axis_index(axis)
    if count % 2:
        done = finish(lax.psum(part.astype(F32), axis))
        return done if choose else (done, done)
    middle = count // 2
    send = lambda value, pairs: lax.ppermute(value, axis, pairs)
    plus = lambda a, b: order.tie(a.astype(F32) + b.astype(F32))
    for k in range(middle - 1):
        pairs = [(k, k + 1), (count - 1 - k, count - 2 - k)]
        got = send(part, pairs)
        yield (part,)
        part = plus(part, got).astype(part.dtype)
    got = send(part, [(middle - 1, middle), (middle, middle - 1)])
    yield (part,)
    done = finish(plus(part, got))
    for k in range(middle - 1, 0, -1):
        got = send(done, [(k, k - 1), (count - 1 - k, count - k)])
        yield (done,)
        if k == 1 and not choose:
            return done, got
        takes = (mine == k - 1) | (mine == count - k)
        done = order.tie(jnp.where(takes, got, done))
    return done if choose else (done, done)


def crossed(order, value, axis, join):
    count = lax.axis_size(axis)
    pairs = lambda distance: [(i, (i + distance) % count) for i in range(count)]
    got = [lax.ppermute(value, axis, pairs(distance)) for distance in range(1, count)]
    yield (value,)
    for other in got:
        value = join(value, other)
    return order.tie(value)


def butterfly(order, value, axis, join):
    for bit in bits_of(axis):
        got = flipped(value, axis, bit)
        yield (value,)
        value = order.tie(join(value, got))
    return value


def bits_of(axis):
    size = lax.axis_size(axis)
    assert size & (size - 1) == 0
    return [1 << k for k in range(size.bit_length() - 1)]


def flipped(value, axis, bit):
    return lax.ppermute(value, axis, [(i, i ^ bit) for i in range(lax.axis_size(axis))])


def joined(one, two):
    state = lax.broadcasted_iota(I32, one.shape, 0) < STATE
    return jnp.where(state, two[STATE : STATE + 1] * one + two, one * two)


def carried(order, payload, axis, backward):
    mine, size = lax.axis_index(axis), lax.axis_size(axis)
    steps = bits_of(axis)
    odd = (mine & 1) == 1
    own = jnp.where(odd, payload[1], payload[0])
    give = jnp.where(odd, payload[0], payload[1])
    got = flipped(give, axis, 1)
    yield (give,)
    is_first = odd if backward else jnp.logical_not(odd)
    got = order.tie(got)
    one, two = jnp.where(is_first, own, got), jnp.where(is_first, got, own)
    total = joined(one, two)
    entering = jnp.broadcast_to((lax.iota(I32, total.shape[0]) >= STATE).astype(F32)[:, None], total.shape)
    for bit in steps[1:]:
        later = ((mine & bit) == 0) if backward else ((mine & bit) != 0)
        last = bit == steps[-1]
        pairs = [(i, i ^ bit) for i in range(size) if not last or bool(i & bit) == backward]
        got = lax.ppermute(total, axis, pairs)
        yield (total,)
        got = order.tie(got)
        entering = jnp.where(later, joined(got, entering), entering)
        if not last:
            total = joined(jnp.where(later, got, total), jnp.where(later, total, got))
    second = joined(entering, one)
    mine_now, other_now = jnp.where(is_first, entering, second), jnp.where(is_first, second, entering)
    back = flipped(other_now, axis, 1)
    yield (other_now,)
    return jnp.stack([jnp.where(odd, back, mine_now), jnp.where(odd, mine_now, back)])


def butterfly_sum(value, axis):
    for bit in bits_of(axis):
        value = value + flipped(value, axis, bit)
    return value


def gathered(value, axis):
    return lax.all_gather(value, axis, axis=1, tiled=True)


def shifted(block, axis, distance):
    devices = range(lax.axis_size(axis))
    route = [(i - distance, i) for i in devices if i - distance in devices]
    return lax.ppermute(block, axis, route)


BRANCH_SCALE = 64.0


def pad_lanes(value, width):
    return jnp.pad(value, [(0, 0)] * (value.ndim - 1) + [(0, width - value.shape[-1])])


def edge_terms(halo, taps):
    ext = jnp.concatenate([jnp.zeros_like(halo), halo], axis=1)
    return sum(taps[CONV - 1 - j] * ext[:, j : j + 8] for j in range(1, CONV))


def per_device(
    residual_in, lengths, norm_gain, gate_projection_weight, head_channels_weight, input_state_pair_weight,
    step_size_weight, x_taps, bc_taps, x_bias, bc_bias, step_bias, decay_log, skip_gain, out_gain,
    output_projection_weight, cotangent,
):
    seqs, slots, width = residual_in.shape
    channels = head_channels_weight.shape[1]
    own = input_state_pair_weight.shape[1]
    heads = step_size_weight.shape[1]
    head_at = lax.axis_index("head")
    count = seqs // GROUPS
    groups = range(GROUPS)
    dot = lambda spec, a, b: jnp.einsum(spec, a, b, preferred_element_type=F32)

    order = Order()
    run = lambda steps: Running(order, steps)

    meta, head, chan, expand = constants(lengths, step_bias, decay_log, skip_gain, out_gain, slots)
    places, limit = meta[:seqs], meta[seqs : 2 * seqs]
    slot = lax.iota(jnp.int32, slots)[:, None]

    before = shifted(residual_in[:, slots - 8 :], "seq", 1)
    pair_rows = gathered(
        jnp.concatenate(
            [input_state_pair_weight.astype(F32), bc_taps, bc_bias[None], jnp.zeros((3, own), F32)], axis=0
        ),
        "head",
    )
    pair_weight = pair_rows[:width].astype(BF16)
    bc_taps_all, bc_bias_all = pair_rows[width : width + CONV], pair_rows[width + CONV : width + CONV + 1]
    step_weight = pad_lanes(step_size_weight, LANES)
    bias = x_bias[None]
    gain_row = norm_gain[None]

    normed, branch_grad, proj, bc_raw, xs, bcs, sc, grad_hidden, cot_peak = ([None] * GROUPS for _ in range(9))
    starts, partials, mixed, states, final, ends = ([None] * GROUPS for _ in range(6))
    hidden, grad_gate, dy, grad_ins, gain_acc = ([None] * GROUPS for _ in range(5))
    branches, sums_of = {}, {}

    def project_of(g):
        normed[g], branch_grad[g], proj[g], grad_hidden[g], cot_peak[g] = project(
            order, meta, residual_in, cotangent, gain_row, gate_projection_weight, head_channels_weight, step_weight,
            output_projection_weight, g * count, count,
        )

    def states_of(g):
        xs[g], bc_raw[g], bcs[g], sc[g], ends[g] = local_states(
            order, meta, proj[g], normed[g], pair_weight, halo_x, halo_bc, x_taps, bias, bc_taps_all, bc_bias_all,
            head, g * count, channels,
        )
        starts[g] = run(carried(order, ends[g], "seq", False))

    def mix_of(g):
        mixed[g], sums, states[g], final[g] = mix(
            order, meta, xs[g], bcs[g], sc[g], starts[g].end(), proj[g], grad_hidden[g], chan
        )
        sums_of[g] = run(crossed(order, sums, "head", lambda a, b: a + b))

    def gate_of(g):
        hidden[g], grad_gate[g], dy[g], grad_end, gain_acc[g] = gate_back(
            order, meta, mixed[g], proj[g], grad_hidden[g], sums_of[g].end(), bcs[g], sc[g], chan
        )
        grad_ins[g] = run(carried(order, grad_end, "seq", True))

    def branch_of(s):
        g, i = divmod(s, count)
        branch = (dot("mq,qh->mh", hidden[g][i], output_projection_weight) * BRANCH_SCALE).astype(F16)
        u = lax.dynamic_index_in_dim(residual_in, places[s], 0, keepdims=False)
        done = lambda total: jnp.where(
            slot < limit[s], u.astype(F32) + total * (1.0 / BRANCH_SCALE), 0.0
        ).astype(BF16)
        branches[s] = run(line_sum(order, branch, "head", done, choose=False))

    def result_of(s, target):
        own_rows, got = branches[s].end()
        return place(order, meta, own_rows[None], got[None], s, seqs, target)

    backs, gps, accs, haccs = [[] for _ in range(GROUPS)], {}, {}, {}
    parts, gbcs, baccs, gain_accs = {}, {}, [], []
    dbc_sums, fixes = {}, {}

    def scale_of():
        largest = jnp.max(functools.reduce(jnp.maximum, cot_peak))
        return run(butterfly(order, jnp.full((8, LANES), largest, F32), "seq", jnp.maximum))

    def back_of(s):
        g, i = divmod(s, count)
        *backs[g], accs[s], haccs[s] = state_back(
            order, meta, i, g * count, proj[g], halo_x, bcs[g], sc[g], dy[g], mixed[g], states[g], final[g],
            grad_ins[g].end(), grad_gate[g], x_taps, bias, head, chan, expand, backs[g] or None,
        )

    def edges_of(g):
        gps[g], _, tail, edge = backs[g]
        fixes[g] = (shifted(edge, "seq", -1), tail[:, -1])
        order.before_next(edge)

    def pair_sum_of(g):
        dbc_sums[g] = run(line_sum(order, order.tie(backs[g][1]), "head", lambda total: total))

    def fix_of(g):
        got, tail = fixes[g]
        fixed = order.tie(tail + edge_terms(got, x_taps)).astype(BF16)
        gps[g] = lax.dynamic_update_slice(gps[g], fixed, (0, slots - 8, channels))

    def part_of(s):
        part = (dot("gl,ol->go", gps[s // count][s % count], weight) * scale[0]).astype(F16)
        parts[s] = run(line_sum(order, part, "head", lambda total: total.astype(F16)))

    def pair_of(g):
        gbc, btail, bedge, bacc = pair_back(
            order, meta, g * count, bc_raw[g], halo_bc, dbc_sums[g].end(), bc_taps_all, bc_bias_all
        )
        baccs.append(bacc)
        gbcs[g] = (gbc, btail, shifted(bedge, "seq", -1))
        order.before_next(bedge)

    def pair_fix(g):
        gbc, btail, got = gbcs[g]
        fixed = order.tie(btail + edge_terms(got, bc_taps_all)).astype(BF16)
        gbcs[g] = lax.dynamic_update_slice(gbc, fixed, (0, slots - 8, 0))

    def finish_of(s, target):
        g, i = divmod(s, count)
        total = parts[s].end().astype(F32) * scale[1]
        target, gain = finish(
            order, meta, total[None], residual_in, branch_grad[g], gbcs[g], pair_weight, gain_row, s, i, target
        )
        gain_accs.append(gain)
        return target

    add = lambda terms: functools.reduce(lambda a, b: a + b, terms)
    tied_dots = lambda spec, pairs: order.tie(add([dot(spec, a, b) for a, b in pairs]))
    project_of(0)
    project_of(1)
    halo_x, halo_bc = edge_halos(order, meta, before, gain_row, head_channels_weight, pair_weight)
    states_of(0)
    peak = scale_of()
    order.fence()
    weight = jnp.concatenate([gate_projection_weight, head_channels_weight, order.tie(step_weight)], axis=1)
    order.before_next(weight)
    starts[0].advance()
    states_of(1)
    peak.advance()
    starts[0].advance()
    order.fence()
    starts[1].advance()
    order.fence()
    starts[0].advance()
    starts[1].advance()
    peak.advance()
    mix_of(0)
    starts[1].advance()
    peak = jnp.maximum(peak.end()[0, 0], 1e-30)
    scale = 0.0625 / peak, 16.0 * peak
    mix_of(1)
    gate_of(0)
    branch_of(0)
    order.fence()
    grad_ins[0].advance()
    gate_of(1)
    grad_ins[0].advance()
    order.fence()
    branch_of(1)
    grad_ins[1].advance()
    order.fence()
    out_grad = tied_dots("yfx,yfw->xw", [(hidden[g], branch_grad[g]) for g in groups])
    order.before_next(out_grad)
    order.fence()
    grad_ins[0].advance()
    grad_ins[1].advance()
    branches[0].advance().pin()
    branch_of(2)
    back_of(0)
    branches[1].advance().pin()
    gate_grad = tied_dots("wji,wjr->ir", [(normed[g], grad_gate[g]) for g in groups])
    order.before_next(gate_grad)
    order.fence()
    grad_ins[1].advance()
    early = lax.psum((out_grad, order.tie(gate_grad)), "seq")
    branch_of(3)
    branches[3].pin()
    back_of(1)
    edges_of(0)
    branches[0].advance()
    branches[2].advance().pin()
    order.fence()
    fix_of(0)
    part_of(0)
    parts[0].pin()
    back_of(2)
    branches[1].advance()
    branches[3].advance().pin()
    result = result_of(0, None)
    pair_sum_of(0)
    back_of(3)
    edges_of(1)
    part_of(1)
    parts[1].pin()
    order.fence()
    parts[0].advance().pin()
    branches[2].advance()
    fix_of(1)
    dbc_sums[0].advance()
    result = result_of(1, result)
    pair_sum_of(1)
    part_of(2)
    parts[2].pin()
    order.fence()
    branches[3].advance()
    result = result_of(2, result)
    part_of(3)
    parts[3].pin()
    order.fence()
    parts[1].advance().pin()
    dbc_sums[0].advance()
    grad_x_weight = tied_dots("wji,wjr->ir", [(normed[g], gps[g][..., channels : 2 * channels]) for g in groups])
    grad_step_weight = tied_dots("wji,wjr->ir", [(normed[g], gps[g][..., 2 * channels :]) for g in groups])
    order.before_next(grad_x_weight, grad_step_weight)
    order.fence()
    dbc_sums[1].advance()
    parts[0].advance()
    result = result_of(3, result)
    out_result, gate_result = order.tie(early[0]), order.tie(early[1])
    order.before_next(out_result, gate_result)
    zero = jnp.clip(out_result[0, 0] + gate_result[0, 0], -1.0, 1.0) * 0.0
    late = lax.psum((grad_x_weight, grad_step_weight + zero), "seq")
    order.fence()
    parts[2].advance().pin()
    order.fence()
    parts[1].advance()
    pair_of(0)
    pair_fix(0)
    grad_input = finish_of(0, None)
    parts[3].advance().pin()
    dbc_sums[1].advance()
    order.fence()
    parts[2].advance()
    grad_input = finish_of(1, grad_input)
    pair_of(1)
    pair_fix(1)
    parts[3].advance()
    grad_pair = add(dot("wji,wjr->ir", normed[g], gbcs[g]) for g in groups)
    grad_own = lax.dynamic_slice(grad_pair, (0, head_at * own), (width, own))
    grad_input = finish_of(2, grad_input)
    x_result, step_result = order.tie(late[0]), late[1]
    order.before_next(x_result)
    grad_input = finish_of(3, grad_input)
    acc = jnp.sum(add(accs.values()).reshape(6, 8, channels), axis=1)
    acc = jnp.concatenate([acc, jnp.sum(add(gain_acc), axis=0)[None]], axis=0)
    hacc = jnp.sum(add(haccs.values()).reshape(2, 8, LANES), axis=1)
    bacc = jnp.sum(add(baccs).reshape(5, 8, 2 * STATE), axis=1)
    flat = jnp.concatenate([acc.reshape(-1), hacc.reshape(-1), bacc.reshape(-1), grad_own.reshape(-1)])
    flat = butterfly_sum(flat.reshape(-1, LANES), "seq").reshape(-1)
    ends_at = [acc.size, acc.size + hacc.size, acc.size + hacc.size + bacc.size]
    acc, hacc, bacc, grad_own = (
        piece.reshape(like.shape) for piece, like in zip(jnp.split(flat, ends_at), (acc, hacc, bacc, grad_own))
    )
    bacc = lax.dynamic_slice(bacc, (0, head_at * own), (5, own))
    gain = butterfly_sum(jnp.sum(add(gain_accs), axis=0).reshape(-1, LANES), "seq").reshape(-1)
    return (
        result,
        grad_input,
        gain,
        gate_result,
        x_result,
        grad_own,
        step_result[:, :heads],
        acc[:CONV],
        bacc[:CONV],
        acc[CONV],
        bacc[CONV],
        hacc[0, :heads],
        hacc[1, :heads],
        jnp.sum(acc[5].reshape(heads, HEAD_DIM), axis=1),
        acc[6],
        out_result,
    )


def solution(mesh):
    return jax.shard_map(
        per_device,
        mesh=mesh,
        in_specs=(
            P(None, "seq", None), P(), P(), P(None, "head"), P(None, "head"), P(None, "head"), P(None, "head"),
            P(None, "head"), P(None, "head"), P("head"), P("head"), P("head"), P("head"), P("head"), P("head"),
            P("head", None), P(None, "seq", None),
        ),
        out_specs=(
            P(None, "seq", None), P(None, "seq", None), P(), P(None, "head"), P(None, "head"), P(None, "head"),
            P(None, "head"), P(None, "head"), P(None, "head"), P("head"), P("head"), P("head"), P("head"),
            P("head"), P("head"), P("head", None),
        ),
        check_vma=False,
    )
```

```python
import functools

import jax
import jax.numpy as jnp
from jax import lax
from jax.experimental import pallas as pl
from jax.experimental.pallas import tpu as pltpu
from jax.sharding import PartitionSpec as P

HEAD_DIM = 64
STATE = 128
CONV = 4
INNER = 3072
CHUNK = 128
ROWS = 256
HALF = 64
LANES = 128
EPSILON = 1e-05
GROUPS = 2
F32 = jnp.float32
BF16 = jnp.bfloat16
F16 = jnp.float16
I32 = jnp.int32
VMEM_LIMIT = 60 * 1024 * 1024


def halves(value):
    high = value.astype(BF16)
    return high, (value - high.astype(F32)).astype(BF16)


def thirds(value):
    high = value.astype(BF16)
    rest = value - high.astype(F32)
    middle = rest.astype(BF16)
    return high, middle, (rest - middle.astype(F32)).astype(BF16)


def mm(a, b, ca=1, cb=0):
    return lax.dot_general(a, b, (((ca,), (cb,)), ((), ())), preferred_element_type=F32)


def dot3(a, b):
    return mm(jnp.concatenate([a[0], a[1]], axis=1), jnp.concatenate([b[0], b[0]], axis=0)) + mm(a[0], b[1])


def dot3_t(a, b):
    n = b[0].shape[0]
    wide = mm(a[0], jnp.concatenate([b[0], b[1]], axis=0), 1, 1)
    return wide[:, :n] + wide[:, n:] + mm(a[1], b[0], 1, 1)


def per_head(value, expand):
    high, low = halves(value)
    return mm(high, expand, 1, 1) + mm(low, expand, 1, 1)


def summed_by(matrix, value):
    out = None
    for part in thirds(value):
        term = mm(matrix, part)
        out = term if out is None else out + term
    return out


def rows8(row):
    return jnp.broadcast_to(row, (8, row.shape[-1]))


def fold8(value):
    return jnp.sum(value.reshape(value.shape[0] // 8, 8, value.shape[1]), axis=0)


def peak8(value):
    return jnp.max(jnp.abs(value).reshape(value.shape[0] // 8, 8, value.shape[1]), axis=0)


def left_half(rows):
    return lax.broadcasted_iota(jnp.int32, (rows, LANES), 1) < HEAD_DIM


def spread_pair(value, pair, left):
    h = 2 * pair
    return jnp.where(left, value[:, h : h + 1], value[:, h + 1 : h + 2])


def spread(value, channels):
    left = left_half(value.shape[0])
    return jnp.concatenate([spread_pair(value, j, left) for j in range(channels // LANES)], axis=1)


def softplus(value):
    small = jnp.exp(-jnp.abs(value))
    one = 1.0 + small
    log = jnp.where(one == 1.0, small, jnp.log(one) * (small / jnp.where(one == 1.0, 1.0, one - 1.0)))
    return jnp.maximum(value, 0.0) + log


def sigmoid(value):
    return 1.0 / (1.0 + jnp.exp(-value))


def conv(ext_ref, taps_ref, bias_ref, start, length, lanes):
    summed = bias_ref[0:1, lanes] + taps_ref[0:1, lanes] * ext_ref[start + 5 : start + 5 + length, lanes]
    for k in range(1, CONV):
        summed = summed + taps_ref[k : k + 1, lanes] * ext_ref[start + 5 + k : start + 5 + k + length, lanes]
    return summed


def conv_back(grad_ref, taps_ref, start, length, lanes):
    raw = taps_ref[CONV - 1 : CONV, lanes] * grad_ref[start : start + length, lanes]
    for j in range(1, CONV):
        raw = raw + taps_ref[CONV - 1 - j : CONV - j, lanes] * grad_ref[start + j : start + j + length, lanes]
    return raw


def as_column(row):
    return jnp.broadcast_to(row, (LANES, LANES)).T


def row_sums(value):
    ones = jnp.ones((8, LANES), BF16)
    parts = thirds(value)
    return mm(ones, parts[0], 1, 1) + (mm(ones, parts[1], 1, 1) + mm(ones, parts[2], 1, 1))


def triangle(length, lower):
    row = lax.broadcasted_iota(jnp.int32, (length, length), 0)
    column = lax.broadcasted_iota(jnp.int32, (length, length), 1)
    return row >= column if lower else row <= column


ANYWHERE = pl.BlockSpec(memory_space=pl.ANY)


class Order:
    def __init__(self):
        self.now, self.pending, self.shape = None, [], (8, 2048)

    def before_next(self, *arrays):
        self.pending += [array for array in arrays if array.dtype != F16]

    def fence(self):
        tokens = self.pending + ([] if self.now is None else [self.now])
        self.pending = []

        def body(*refs):
            refs[-1][...] = jnp.zeros_like(refs[-1])

        self.now = pl.pallas_call(
            body,
            in_specs=[ANYWHERE] * len(tokens),
            out_shape=SHAPE(self.shape, F32),
            compiler_params=pltpu.CompilerParams(vmem_limit_bytes=VMEM_LIMIT),
            name="fence",
        )(*tokens)

    def tie(self, value):
        if self.now is None:
            return value
        zeros = lax.slice(self.now, (0, 0), (1, value.shape[-1])).astype(value.dtype)
        return value + zeros.reshape((1,) * (value.ndim - 1) + (value.shape[-1],))

    def call(self, kernel, operands, *, meta, grid, in_specs, out_specs, out_shape, scratch=(), flops, moved, name, aliases=None):
        tokens = self.pending + ([] if self.now is None else [self.now])
        inputs, outputs = len(operands), len(out_shape)
        self.pending = []

        def body(meta_ref, *refs):
            last = inputs + len(tokens) + outputs
            refs[last][...] = jnp.zeros_like(refs[last])
            kernel(meta_ref, *refs[:inputs], *refs[inputs + len(tokens) : last], *refs[last + 1 :])

        result = pl.pallas_call(
            body,
            grid_spec=pltpu.PrefetchScalarGridSpec(
                num_scalar_prefetch=1,
                grid=grid,
                in_specs=list(in_specs) + [ANYWHERE] * len(tokens),
                out_specs=list(out_specs) + [whole(self.shape)],
                scratch_shapes=list(scratch),
            ),
            out_shape=list(out_shape) + [SHAPE(self.shape, F32)],
            input_output_aliases=aliases or {},
            compiler_params=pltpu.CompilerParams(
                vmem_limit_bytes=VMEM_LIMIT, dimension_semantics=("arbitrary",) * len(grid)
            ),
            cost_estimate=pl.CostEstimate(flops=int(flops), bytes_accessed=int(moved), transcendentals=0),
            name=name,
        )(meta, *operands, *tokens)
        self.now = result[-1]
        return result[:-1]


def constants_kernel(lengths_ref, step_bias_ref, decay_ref, skip_ref, out_gain_ref, meta_ref, head_ref, chan_ref, expand_ref, *, slots):
    seqs, heads = lengths_ref.shape[0], step_bias_ref.shape[1]
    channels = out_gain_ref.shape[1]
    place, least = jnp.int32(0), lengths_ref[0]
    for s in range(1, seqs):
        shorter = lengths_ref[s] < least
        place, least = jnp.where(shorter, s, place), jnp.where(shorter, lengths_ref[s], least)
    first = lax.axis_index("seq") * slots
    for s in range(seqs):
        source = jnp.where(place == s, seqs - 1, s) if s < seqs - 1 else place
        meta_ref[s] = source
        meta_ref[seqs + s] = lengths_ref[source] - first
    mine, count = lax.axis_index("head"), lax.axis_size("head")
    meta_ref[2 * seqs] = jnp.where((mine == 0) | (mine == count - 1), 1, 0)
    lane = lax.broadcasted_iota(jnp.int32, (8, LANES), 1)
    row = lax.broadcasted_iota(jnp.int32, (8, LANES), 0)
    pad = lambda ref: jnp.concatenate([ref[...], jnp.zeros((1, LANES - heads), F32)], axis=1)
    head_ref[...] = jnp.zeros((8, LANES), F32)
    head_ref[0:1, :] = pad(step_bias_ref)
    head_ref[1:2, :] = pad(decay_ref)
    chan_ref[...] = jnp.zeros_like(chan_ref)
    chan_ref[0:1, :] = spread(rows8(pad(skip_ref)), channels)[0:1, :]
    chan_ref[1:2, :] = out_gain_ref[...]
    head_of = lax.broadcasted_iota(jnp.int32, (LANES, channels), 1) // HEAD_DIM
    expand_ref[...] = jnp.where(head_of == lax.broadcasted_iota(jnp.int32, (LANES, channels), 0), 1.0, 0.0).astype(BF16)


def normalized(rows, gain):
    u = rows.astype(F32)
    scale = lax.rsqrt(jnp.mean(u * u, axis=-1, keepdims=True) + EPSILON)
    return (u * scale * gain).astype(BF16)


def project_kernel(
    meta_ref, u_ref, cot_ref, gain_ref, gate_ref, x_ref, step_ref, out_ref, normed_ref, branch_ref, proj_ref, gh_ref,
    peak_ref, input_ref, *, first
):
    @pl.when((pl.program_id(1) == 0) & (pl.program_id(0) == 0))
    def _():
        peak_ref[...] = jnp.zeros_like(peak_ref)

    rows, channels = u_ref.shape[0], gate_ref.shape[1]
    normed = normalized(u_ref[...], gain_ref[...])
    normed_ref[...] = normed
    at = pl.program_id(1) * rows + lax.broadcasted_iota(jnp.int32, cot_ref.shape, 0)
    live = at < meta_ref[4 + first + pl.program_id(0)]
    input_ref[...] = jnp.where(live, u_ref[...].astype(F32), 0.0).astype(BF16)
    branch = jnp.where(live, cot_ref[...].astype(F32), 0.0)
    peak_ref[...] = jnp.maximum(peak_ref[...], peak8(branch))
    branch = branch.astype(BF16)
    branch_ref[...] = branch
    proj_ref[:, :channels] = mm(normed, gate_ref[...])
    proj_ref[:, channels : 2 * channels] = mm(normed, x_ref[...])
    proj_ref[:, 2 * channels :] = mm(normed, step_ref[...])
    gh_ref[...] = mm(branch, out_ref[...], 1, 1)


def edge_kernel(meta_ref, before_ref, gain_ref, x_ref, pair_ref, xhalo_ref, bchalo_ref):
    seqs, rows, width = before_ref.shape
    normed = normalized(before_ref[...].reshape(seqs * rows, width), gain_ref[...])
    xhalo_ref[...] = mm(normed, x_ref[...]).reshape(xhalo_ref.shape)
    bchalo_ref[...] = mm(normed, pair_ref[...]).reshape(bchalo_ref.shape)


def local_state_kernel(
    meta_ref, x_ref, xhalo_ref, normed_ref, pair_ref, bchalo_ref, step_ref, taps_ref, bias_ref, btaps_ref, bbias_ref,
    head_ref, xs_ref, raw_ref, bcs_ref, sc_ref, end_ref, xe, be, state, total,
):
    c, rows = pl.program_id(1), x_ref.shape[0]
    channels = x_ref.shape[1]

    @pl.when(c == 0)
    def _():
        xe[0:8, :] = xhalo_ref[...]
        be[0:8, :] = bchalo_ref[...]
        state[...] = jnp.zeros_like(state)
        total[...] = jnp.zeros_like(total)

    xe[8 : 8 + rows, :] = x_ref[...]
    raw = mm(normed_ref[...], pair_ref[...])
    raw_ref[...] = raw
    be[8 : 8 + rows, :] = raw
    lower = triangle(CHUNK, True).astype(BF16)
    left = left_half(CHUNK)
    lane = lax.broadcasted_iota(I32, (CHUNK, LANES), 1)
    for at in range(0, rows, CHUNK):
        here = slice(at, at + CHUNK)
        for lanes in (slice(0, STATE), slice(STATE, 2 * STATE)):
            pb = conv(be, btaps_ref, bbias_ref, at, CHUNK, lanes)
            bcs_ref[here, lanes] = pb * sigmoid(pb)
        step = softplus(step_ref[here, :] + head_ref[0:1, :])
        cum = summed_by(lower, -step * jnp.exp(head_ref[1:2, :]))
        sc_ref[here, :] = jnp.where(lane < HALF, step, pltpu.roll(cum, HALF, 1))
        end = cum[CHUNK - 1 : CHUNK, :]
        fading = step * jnp.exp(end - cum)
        keep = spread(rows8(jnp.exp(end)), channels)
        bt2 = halves(bcs_ref[here, :STATE].T)
        for pair in range(channels // LANES):
            lanes = slice(pair * LANES, (pair + 1) * LANES)
            p = conv(xe, taps_ref, bias_ref, at, CHUNK, lanes)
            xs = p * sigmoid(p)
            xs_ref[here, lanes] = xs
            weighted = halves(xs * spread_pair(fading, pair, left))
            state[:, lanes] = keep[0:1, lanes] * state[:, lanes] + dot3(bt2, weighted)
        total[...] += rows8(end)
    xe[0:8, :] = xe[rows : rows + 8, :]
    be[0:8, :] = be[rows : rows + 8, :]

    @pl.when(c == pl.num_programs(1) - 1)
    def _():
        end_ref[0:STATE, :] = state[...]
        end_ref[STATE : STATE + 8, :] = spread(jnp.exp(total[...]), channels)


def mix_kernel(
    meta_ref, xs_ref, bcs_ref, sc_ref, start_ref, gate_ref, gh_ref, chan_ref,
    mixed_ref, red_ref, states_ref, final_ref, state,
):
    c, rows = pl.program_id(1), xs_ref.shape[0]
    channels = xs_ref.shape[1]

    @pl.when(c == 0)
    def _():
        state[...] = start_ref[...]

    lower = triangle(CHUNK, True)
    left = left_half(CHUNK)
    zero = jnp.zeros((CHUNK, LANES), BF16)
    for at in range(0, rows, CHUNK):
        here = slice(at, at + CHUNK)
        entering = state[...]
        states_ref[at // CHUNK] = entering
        sc = sc_ref[here, :]
        sc_t = sc.T
        b2, c2 = halves(bcs_ref[here, :STATE]), halves(bcs_ref[here, STATE:])
        bt2 = halves(bcs_ref[here, :STATE].T)
        scores = dot3_t(c2, b2)
        carried = dot3(c2, halves(entering))
        end_full = spread(rows8(pltpu.roll(sc, HALF, 1)[CHUNK - 1 : CHUNK, :]), channels)
        sq = jnp.zeros((CHUNK, LANES), F32)
        dt = jnp.zeros((CHUNK, LANES), F32)
        for pair in range(channels // LANES):
            lanes = slice(pair * LANES, (pair + 1) * LANES)
            xs = xs_ref[here, lanes]
            weighted = xs * spread_pair(sc, pair, left)
            high, low = halves(weighted)
            stacked, columns = [], []
            for h in (HALF + 2 * pair, HALF + 2 * pair + 1):
                column = jnp.broadcast_to(sc[:, h : h + 1], (CHUNK, LANES))
                columns.append(column)
                mixing = jnp.where(lower, jnp.exp(column - sc_t[h : h + 1, :]), 0.0) * scores
                stacked.append(jnp.concatenate(halves(mixing), axis=1))
            right = jnp.concatenate(
                [jnp.concatenate([high, low], axis=1), jnp.concatenate([high, zero], axis=1)], axis=0
            )
            out = mm(jnp.concatenate(stacked, axis=0), right)
            out = out[:, :LANES] + out[:, LANES:]
            cum_full = jnp.where(left, columns[0], columns[1])
            mixed = (
                jnp.where(left, out[:CHUNK], out[CHUNK:])
                + carried[:, lanes] * jnp.exp(cum_full)
                + chan_ref[0:1, lanes] * xs
            )
            mixed_ref[here, lanes] = mixed
            gate = gate_ref[here, lanes]
            gated = mixed * (gate * sigmoid(gate))
            sq = sq + gated * gated
            dt = dt + gated * (gh_ref[here, lanes] * chan_ref[1:2, lanes])
            tail = end_full[0:1, lanes]
            later = halves(weighted * jnp.exp(tail - cum_full))
            state[:, lanes] = jnp.exp(tail) * state[:, lanes] + dot3(bt2, later)
        row = lax.broadcasted_iota(I32, (8, CHUNK), 0)
        red_ref[:, here] = jnp.where(row == 0, row_sums(sq), row_sums(dt))

    @pl.when(c == pl.num_programs(1) - 1)
    def _():
        final_ref[...] = state[...]


def gate_back_kernel(
    meta_ref, mixed_ref, gate_ref, gh_ref, row_ref, bcs_ref, sc_ref, chan_ref,
    hidden_ref, ggate_ref, dy_ref, gend_ref, acc_ref, grad, total, *, first
):
    c, rows = pl.program_id(1), mixed_ref.shape[0]
    start = (pl.num_programs(1) - 1 - c) * rows
    limit = meta_ref[4 + first + pl.program_id(0)]
    channels = mixed_ref.shape[1]

    @pl.when(c == 0)
    def _():
        grad[...] = jnp.zeros_like(grad)
        total[...] = jnp.zeros_like(total)

    @pl.when((c == 0) & (pl.program_id(0) == 0))
    def _():
        acc_ref[...] = jnp.zeros_like(acc_ref)

    left = left_half(CHUNK)
    for at in reversed(range(0, rows, CHUNK)):
        here = slice(at, at + CHUNK)
        cum = pltpu.roll(sc_ref[here, :], HALF, 1)
        ct2 = halves(bcs_ref[here, STATE:].T)
        keep = spread(rows8(jnp.exp(cum[CHUNK - 1 : CHUNK, :])), channels)
        grown = jnp.exp(cum)
        live = start + at + lax.broadcasted_iota(I32, (CHUNK, LANES), 0) < limit
        squares, dots = as_column(row_ref[0:1, here]), as_column(row_ref[1:2, here])
        r = lax.rsqrt(squares * (1.0 / INNER) + EPSILON)
        pull = r * r * r * dots * (1.0 / INNER)
        for pair in range(channels // LANES):
            lanes = slice(pair * LANES, (pair + 1) * LANES)
            mixed, gate, gh = mixed_ref[here, lanes], gate_ref[here, lanes], gh_ref[here, lanes]
            out_gain = chan_ref[1:2, lanes]
            sig = sigmoid(gate)
            silu = gate * sig
            gated = mixed * silu
            normal = gated * r
            hidden_ref[here, lanes] = jnp.where(live, normal * out_gain, 0.0).astype(BF16)
            acc_ref[:, lanes] += fold8(gh * normal)
            grad_gated = r * (gh * out_gain) - gated * pull
            dy = grad_gated * silu
            dy_ref[here, lanes] = dy
            ggate_ref[here, lanes] = (grad_gated * mixed * (sig * (1.0 + gate * (1.0 - sig)))).astype(BF16)
            grad[:, lanes] = keep[0:1, lanes] * grad[:, lanes] + dot3(
                ct2, halves(dy * spread_pair(grown, pair, left))
            )
        total[...] += rows8(cum[CHUNK - 1 : CHUNK, :])

    @pl.when(c == pl.num_programs(1) - 1)
    def _():
        gend_ref[0:STATE, :] = grad[...]
        gend_ref[STATE : STATE + 8, :] = spread(jnp.exp(total[...]), channels)


def state_back_kernel(
    meta_ref, x_ref, xprev_ref, xhalo_ref, bcs_ref, sc_ref, step_ref, dy_ref, mixed_ref, states_ref, final_ref,
    gin_ref, ggate_ref, taps_ref, bias_ref, head_ref, chan_ref, expand_ref, *refs
):
    gp_ref, dbc_ref, tail_ref, first_ref, acc_ref, hacc_ref = refs[-15:-9]
    xe, ge, grad, flux, wide, wlow, dhigh, dlow, sums = refs[-9:]
    c, rows = pl.program_id(1), x_ref.shape[0]
    blocks = pl.num_programs(1)
    channels = x_ref.shape[1]
    expand = expand_ref[...]

    @pl.when((c == 0) & (pl.program_id(0) == 0))
    def _():
        acc_ref[...] = jnp.zeros_like(acc_ref)
        hacc_ref[...] = jnp.zeros_like(hacc_ref)

    @pl.when(c == 0)
    def _():
        grad[...] = gin_ref[...]
        ending = per_head(fold8(grad[...] * final_ref[...]), expand)
        flux[...] = rows8(jnp.sum(ending, axis=0, keepdims=True))
        ge[rows : rows + 8, :] = jnp.zeros((8, channels), F32)

    @pl.when(c != 0)
    def _():
        ge[rows : rows + 8, :] = ge[0:8, :]

    @pl.when(c == blocks - 1)
    def _():
        xe[0:8, :] = xhalo_ref[...]

    @pl.when(c != blocks - 1)
    def _():
        xe[0:8, :] = xprev_ref[...]

    xe[8 : 8 + rows, :] = x_ref[...]
    gp_ref[:, :channels] = ggate_ref[...]
    upper = triangle(CHUNK, False)
    left = left_half(CHUNK)
    zero = jnp.zeros((CHUNK, LANES), BF16)
    right_lanes = jnp.logical_not(left)
    for at in reversed(range(0, rows, CHUNK)):
        here = slice(at, at + CHUNK)
        sc = sc_ref[here, :]
        sc_t = sc.T
        cum = pltpu.roll(sc, HALF, 1)
        end_full = spread(rows8(cum[CHUNK - 1 : CHUNK, :]), channels)
        b2, c2 = halves(bcs_ref[here, :STATE]), halves(bcs_ref[here, STATE:])
        ct2 = halves(bcs_ref[here, STATE:].T)
        scores_t = dot3_t(b2, c2)
        leaving2 = halves(grad[...])
        pulled = dot3(b2, leaving2)
        dscores_t = jnp.zeros((CHUNK, CHUNK), F32)
        for pair in range(channels // LANES):
            lanes = slice(pair * LANES, (pair + 1) * LANES)
            p = conv(xe, taps_ref, bias_ref, at, CHUNK, lanes)
            sig = sigmoid(p)
            xs = p * sig
            slope = sig * (1.0 + p * (1.0 - sig))
            step_full = spread_pair(sc, pair, left)
            weighted = xs * step_full
            wh, wl = halves(weighted)
            dy = dy_ref[here, lanes]
            dh, dl = halves(dy)
            mine = [
                (jnp.where(keep_lane, wh, zero), jnp.where(keep_lane, wl, zero)) for keep_lane in (left, right_lanes)
            ]
            wide_rows = jnp.concatenate([jnp.concatenate(pieces, axis=1) for pieces in mine], axis=0)
            high_rows = jnp.concatenate([pieces[0] for pieces in mine], axis=0)
            products = mm(wide_rows, jnp.concatenate([dh, dh], axis=1), 1, 1) + mm(high_rows, dl, 1, 1)
            stacked, columns = [], []
            for side, h in enumerate((HALF + 2 * pair, HALF + 2 * pair + 1)):
                column = jnp.broadcast_to(sc[:, h : h + 1], (CHUNK, LANES))
                columns.append(column)
                kern = jnp.where(upper, jnp.exp(sc_t[h : h + 1, :] - column), 0.0)
                dscores_t = dscores_t + kern * products[side * CHUNK : (side + 1) * CHUNK]
                stacked.append(jnp.concatenate(halves(kern * scores_t), axis=1))
            right = jnp.concatenate(
                [jnp.concatenate([dh, dl], axis=1), jnp.concatenate([dh, zero], axis=1)], axis=0
            )
            out = mm(jnp.concatenate(stacked, axis=0), right)
            out = out[:, :LANES] + out[:, LANES:]
            cum_full = jnp.where(left, columns[0], columns[1])
            fade = jnp.exp(end_full[0:1, lanes] - cum_full)
            dxw = jnp.where(left, out[:CHUNK], out[CHUNK:]) + pulled[:, lanes] * fade
            grad_xs = step_full * dxw + chan_ref[0:1, lanes] * dy
            wide[:, lanes], wlow[:, lanes] = halves(weighted * fade)
            gh, gl = halves(dy * jnp.exp(cum_full))
            dhigh[:, lanes], dlow[:, lanes] = gh, gl
            keep = jnp.exp(end_full[0:1, lanes])
            grad[:, lanes] = keep * grad[:, lanes] + dot3(ct2, (gh, gl))
            sums[0:CHUNK, lanes] = xs * dxw
            sums[CHUNK:, lanes] = dy * mixed_ref[here, lanes] - xs * grad_xs
            grad_p = grad_xs * slope
            ge[here, lanes] = grad_p
            for k in range(CONV):
                acc_ref[8 * k : 8 * k + 8, lanes] += fold8(grad_p * xe[at + 5 + k : at + 5 + k + CHUNK, lanes])
            acc_ref[32:40, lanes] += fold8(grad_p)
            acc_ref[40:48, lanes] += fold8(dy * xs)
            raw = conv_back(ge, taps_ref, at, CHUNK, lanes)
            gp_ref[here, channels + pair * LANES : channels + (pair + 1) * LANES] = raw.astype(BF16)
            if at == rows - CHUNK:
                tail_ref[:, lanes] = raw[CHUNK - 8 :, :]
        entering2 = halves(states_ref[at // CHUNK])
        dscores2 = halves(dscores_t)
        dscores_back = halves(dscores_t.T)
        dbc_ref[here, :STATE] = dot3(dscores2, c2) + dot3_t((wide[...], wlow[...]), leaving2)
        dbc_ref[here, STATE:] = dot3(dscores_back, b2) + dot3_t((dhigh[...], dlow[...]), entering2)
        both = per_head(sums[...], expand)
        grad_rate = summed_by(upper.astype(BF16), both[CHUNK:]) + flux[0:1, :]
        flux[...] = rows8(grad_rate[0:1, :])
        rate_of = jnp.exp(head_ref[1:2, :])
        grad_step = both[:CHUNK] - rate_of * grad_rate
        grad_raw = grad_step * sigmoid(step_ref[here, :] + head_ref[0:1, :])
        hacc_ref[0:8, :] += fold8(grad_raw)
        hacc_ref[8:16, :] += fold8(-rate_of * jnp.where(lax.broadcasted_iota(I32, sc.shape, 1) < HALF, sc, 0.0) * grad_rate)
        gp_ref[here, 2 * channels :] = grad_raw.astype(BF16)

    @pl.when(c == blocks - 1)
    def _():
        first_ref[...] = ge[0:8, :]


def pair_back_kernel(
    meta_ref, raw_ref, halo_ref, g_ref, taps_ref, bias_ref, out_ref, tail_ref, first_ref, acc_ref, xe, ge
):
    length, channels = raw_ref.shape

    @pl.when(pl.program_id(0) == 0)
    def _():
        acc_ref[...] = jnp.zeros_like(acc_ref)

    xe[0:8, :] = halo_ref[...]
    xe[8 : 8 + length, :] = raw_ref[...]
    ge[length : length + 8, :] = jnp.zeros((8, channels), F32)
    for at in range(0, length, CHUNK):
        here = slice(at, at + CHUNK)
        for half in range(2):
            lanes = slice(half * STATE, (half + 1) * STATE)
            p = conv(xe, taps_ref, bias_ref, at, CHUNK, lanes)
            sig = sigmoid(p)
            grad_p = g_ref[here, lanes] * (sig * (1.0 + p * (1.0 - sig)))
            ge[here, lanes] = grad_p
            for k in range(CONV):
                acc_ref[8 * k : 8 * k + 8, lanes] += fold8(grad_p * xe[at + 5 + k : at + 5 + k + CHUNK, lanes])
            acc_ref[32:40, lanes] += fold8(grad_p)
    for at in range(0, length, CHUNK):
        for lanes in (slice(0, STATE), slice(STATE, 2 * STATE)):
            raw = conv_back(ge, taps_ref, at, CHUNK, lanes)
            out_ref[at : at + CHUNK, lanes] = raw.astype(BF16)
            if at == length - CHUNK:
                tail_ref[:, lanes] = raw[CHUNK - 8 :, :]
    first_ref[...] = ge[0:8, :]


def finish_kernel(meta_ref, gn_ref, u_ref, branch_ref, gbc_ref, weight_ref, gain_ref, *refs):
    out_ref, acc_ref = refs[-2:]

    @pl.when((pl.program_id(1) == 0) & (pl.program_id(0) == 0))
    def _():
        acc_ref[...] = jnp.zeros_like(acc_ref)

    u = u_ref[...].astype(F32)
    scale = lax.rsqrt(jnp.mean(u * u, axis=-1, keepdims=True) + EPSILON)
    grad = gn_ref[...] + mm(gbc_ref[...], weight_ref[...], 1, 1)
    normal = u * scale
    acc_ref[...] += fold8(grad * normal)
    w = grad * gain_ref[...]
    pull = scale * jnp.mean(w * normal, axis=-1, keepdims=True)
    out_ref[...] = scale * w - normal * pull + branch_ref[...].astype(F32)


def place_kernel(meta_ref, own_ref, got_ref, *refs, takes_at):
    out_ref = refs[-1]
    takes = meta_ref[takes_at] == 1

    @pl.when(takes)
    def _():
        out_ref[...] = got_ref[...]

    @pl.when(jnp.logical_not(takes))
    def _():
        out_ref[...] = own_ref[...]


SHAPE = jax.ShapeDtypeStruct


def whole(shape):
    return pl.BlockSpec(shape, lambda s, c, meta: (0,) * len(shape))


def per_seq(rows, width):
    return pl.BlockSpec((None, rows, width), lambda s, c, meta: (s, 0, 0))


def forward_rows(width, column):
    return pl.BlockSpec((None, ROWS, width), lambda s, c, meta: (s, c, column))


def constants(lengths, step_bias, decay_log, skip_gain, out_gain, slots):
    seqs, channels = lengths.shape[0], out_gain.shape[0]
    row = lambda value: value[None]
    smem = pl.BlockSpec(memory_space=pltpu.SMEM)
    vmem = pl.BlockSpec(memory_space=pltpu.VMEM)
    return pl.pallas_call(
        functools.partial(constants_kernel, slots=slots),
        in_specs=[smem] + [vmem] * 4,
        out_specs=[smem, vmem, vmem, vmem],
        out_shape=[
            SHAPE((2 * seqs + 1,), jnp.int32), SHAPE((8, LANES), F32), SHAPE((8, channels), F32),
            SHAPE((LANES, channels), BF16),
        ],
        name="constants",
    )(lengths, row(step_bias), row(decay_log), row(skip_gain), row(out_gain))


def project(order, meta, residual_in, cotangent, gain, gate, x, step, out, first, count):
    seqs, slots, width = residual_in.shape
    channels = gate.shape[1]
    rows = 256
    placed = pl.BlockSpec((None, rows, width), lambda s, c, meta: (meta[s + first], c, 0))
    plain = lambda wide: pl.BlockSpec((None, rows, wide), lambda s, c, meta: (s, c, 0))
    wide = 2 * channels + LANES
    return order.call(
        functools.partial(project_kernel, first=first),
        (residual_in, cotangent, gain, gate, x, step, out),
        meta=meta,
        grid=(count, slots // rows),
        in_specs=[placed, placed] + [whole(a.shape) for a in (gain, gate, x, step, out)],
        out_specs=[plain(width), plain(width), plain(wide), plain(channels), whole((8, width)), plain(width)],
        out_shape=[
            SHAPE((count, slots, width), BF16), SHAPE((count, slots, width), BF16),
            SHAPE((count, slots, wide), F32), SHAPE((count, slots, channels), F32), SHAPE((8, width), F32),
            SHAPE((count, slots, width), BF16),
        ],
        flops=2 * count * slots * width * (wide + channels),
        moved=count * slots * (width * 8 + wide * 4),
        name="project",
    )


def edge_halos(order, meta, before, gain, x, pair):
    seqs = before.shape[0]
    operands = (before, gain, x, pair)
    shapes = [(seqs, 8, x.shape[1]), (seqs, 8, pair.shape[1])]
    return order.call(
        edge_kernel,
        operands,
        meta=meta,
        grid=(1, 1),
        in_specs=[whole(a.shape) for a in operands],
        out_specs=[whole(a) for a in shapes],
        out_shape=[SHAPE(a, F32) for a in shapes],
        flops=1e8,
        moved=4e6,
        name="edge_halos",
    )


def local_states(order, meta, proj, normed, pair, halo_x, halo_bc, taps, bias, btaps, bbias, head, first, channels):
    count, slots, _ = proj.shape
    placed = lambda width: pl.BlockSpec((None, 8, width), lambda s, c, meta: (meta[first + s], 0, 0))
    return order.call(
        local_state_kernel,
        (proj, halo_x, normed, pair, halo_bc, proj, taps, bias, btaps, bbias, head),
        meta=meta,
        grid=(count, slots // ROWS),
        in_specs=[
            forward_rows(channels, 1), placed(channels), forward_rows(normed.shape[2], 0), whole(pair.shape),
            placed(2 * STATE),
            forward_rows(LANES, 2 * channels // LANES), whole(taps.shape), whole(bias.shape), whole(btaps.shape),
            whole(bbias.shape), whole(head.shape),
        ],
        out_specs=[
            forward_rows(channels, 0), forward_rows(2 * STATE, 0), forward_rows(2 * STATE, 0),
            forward_rows(LANES, 0), per_seq(STATE + 8, channels),
        ],
        out_shape=[
            SHAPE((count, slots, channels), F32), SHAPE((count, slots, 2 * STATE), F32),
            SHAPE((count, slots, 2 * STATE), F32),
            SHAPE((count, slots, LANES), F32), SHAPE((count, STATE + 8, channels), F32),
        ],
        scratch=[
            pltpu.VMEM((ROWS + 8, channels), F32), pltpu.VMEM((ROWS + 8, 2 * STATE), F32),
            pltpu.VMEM((STATE, channels), F32), pltpu.VMEM((8, LANES), F32),
        ],
        flops=count * 4e9,
        moved=count * slots * channels * 8,
        name="local_states",
    )


def mix(order, meta, xs, bcs, sc, start, proj, grad_hidden, chan):
    count, slots, channels = xs.shape
    chunks = slots // CHUNK
    return order.call(
        mix_kernel,
        (xs, bcs, sc, start, proj, grad_hidden, chan),
        meta=meta,
        grid=(count, slots // ROWS),
        in_specs=[
            forward_rows(channels, 0), forward_rows(2 * STATE, 0), forward_rows(LANES, 0),
            per_seq(STATE, channels),
            forward_rows(channels, 0), forward_rows(channels, 0), whole(chan.shape),
        ],
        out_specs=[
            forward_rows(channels, 0), pl.BlockSpec((None, 8, ROWS), lambda s, c, meta: (s, 0, c)),
            pl.BlockSpec((None, ROWS // CHUNK, STATE, channels), lambda s, c, meta: (s, c, 0, 0)),
            per_seq(STATE, channels),
        ],
        out_shape=[
            SHAPE((count, slots, channels), F32), SHAPE((count, 8, slots), F32),
            SHAPE((count, chunks, STATE, channels), F32), SHAPE((count, STATE, channels), F32),
        ],
        scratch=[pltpu.VMEM((STATE, channels), F32)],
        flops=count * 6e9,
        moved=count * slots * channels * 20,
        name="mix",
    )


def gate_back(order, meta, first, mixed, proj, grad_hidden, rows, bcs, sc, chan):
    count, slots, channels = mixed.shape
    chunks = slots // ROWS
    row = lambda width, column: pl.BlockSpec(
        (None, ROWS, width), lambda s, c, meta: (s, chunks - 1 - c, column)
    )
    return order.call(
        functools.partial(gate_back_kernel, first=first),
        (mixed, proj, grad_hidden, rows, bcs, sc, chan),
        meta=meta,
        grid=(count, chunks),
        in_specs=[
            row(channels, 0), row(channels, 0), row(channels, 0),
            pl.BlockSpec((None, 8, ROWS), lambda s, c, meta: (s, 0, chunks - 1 - c)), row(2 * STATE, 0),
            row(LANES, 0), whole(chan.shape),
        ],
        out_specs=[
            row(channels, 0), row(channels, 0), row(channels, 0), per_seq(STATE + 8, channels),
            whole((8, channels)),
        ],
        out_shape=[
            SHAPE((count, slots, channels), BF16), SHAPE((count, slots, channels), BF16),
            SHAPE((count, slots, channels), F32), SHAPE((count, STATE + 8, channels), F32),
            SHAPE((8, channels), F32),
        ],
        scratch=[pltpu.VMEM((STATE, channels), F32), pltpu.VMEM((8, LANES), F32)],
        flops=count * 4e9,
        moved=count * slots * channels * 20,
        name="gate_back",
    )


def state_back(
    order, meta, at, first, proj, halo_x, bcs, sc, dy, mixed, states, final, grad_in, grad_gate, taps, bias, head, chan, expand,
    earlier,
):
    count, slots, channels = mixed.shape
    chunks = slots // ROWS
    tiles = ROWS // 8
    row = lambda width, column, s=at: pl.BlockSpec(
        (None, ROWS, width), lambda _, c, meta: (s, chunks - 1 - c, column)
    )
    only = lambda rows, width, s=at: pl.BlockSpec((None, rows, width), lambda _, c, meta: (s, 0, 0))
    before = pl.BlockSpec(
        (None, 8, channels), lambda _, c, meta: (at, jnp.maximum((chunks - 1 - c) * tiles - 1, 0), 1)
    )
    tail = pl.BlockSpec((None, None, 8, channels), lambda _, c, meta: (at, chunks - 1 - c, 0, 0))
    extra = () if earlier is None else tuple(earlier)
    return order.call(
        state_back_kernel,
        (
            proj, proj, halo_x, bcs, sc, proj, dy, mixed, states, final, grad_in, grad_gate, taps, bias, head, chan,
            expand,
        ) + extra,
        meta=meta,
        grid=(1, chunks),
        in_specs=[
            row(channels, 1), before,
            pl.BlockSpec((None, 8, channels), lambda _, c, meta: (meta[first + at], 0, 0)),
            row(2 * STATE, 0), row(LANES, 0),
            row(LANES, 2 * channels // LANES), row(channels, 0), row(channels, 0),
            pl.BlockSpec((None, ROWS // CHUNK, STATE, channels), lambda _, c, meta: (at, chunks - 1 - c, 0, 0)),
            only(STATE, channels),
            only(STATE, channels),
            row(channels, 0),
            whole(taps.shape), whole(bias.shape), whole(head.shape), whole(chan.shape), whole(expand.shape),
        ] + [ANYWHERE] * len(extra),
        out_specs=[
            row(2 * channels + LANES, 0), row(2 * STATE, 0), tail, only(8, channels),
            whole((48, channels)), whole((16, LANES)),
        ],
        out_shape=[
            SHAPE((count, slots, 2 * channels + LANES), BF16), SHAPE((count, slots, 2 * STATE), F32),
            SHAPE((count, chunks, 8, channels), F32), SHAPE((count, 8, channels), F32),
            SHAPE((48, channels), F32), SHAPE((16, LANES), F32),
        ],
        scratch=[
            pltpu.VMEM((ROWS + 8, channels), F32), pltpu.VMEM((ROWS + 8, channels), F32),
            pltpu.VMEM((STATE, channels), F32), pltpu.VMEM((8, LANES), F32),
            pltpu.VMEM((CHUNK, channels), BF16), pltpu.VMEM((CHUNK, channels), BF16),
            pltpu.VMEM((CHUNK, channels), BF16), pltpu.VMEM((CHUNK, channels), BF16),
            pltpu.VMEM((2 * CHUNK, channels), F32),
        ],
        aliases={18 + i: i for i in range(4)} if extra else None,
        flops=12e9,
        moved=slots * channels * 24,
        name="state_back",
    )


def pair_back(order, meta, first, raw, halo, grad, taps, bias):
    count, slots, channels = raw.shape
    placed = pl.BlockSpec((None, 8, channels), lambda s, c, meta: (meta[first + s], 0, 0))
    return order.call(
        pair_back_kernel,
        (raw, halo, grad, taps, bias),
        meta=meta,
        grid=(count, 1),
        in_specs=[
            per_seq(slots, channels), placed, per_seq(slots, channels), whole(taps.shape), whole(bias.shape),
        ],
        out_specs=[
            per_seq(slots, channels), per_seq(8, channels), per_seq(8, channels), whole((40, channels)),
        ],
        out_shape=[
            SHAPE((count, slots, channels), BF16), SHAPE((count, 8, channels), F32),
            SHAPE((count, 8, channels), F32), SHAPE((40, channels), F32),
        ],
        scratch=[pltpu.VMEM((slots + 8, channels), F32), pltpu.VMEM((slots + 8, channels), F32)],
        flops=count * 1e9,
        moved=count * slots * channels * 10,
        name="pair_back",
    )


def finish(order, meta, grad_normed, residual_in, branch, gbc, weight, gain, at, local, target):
    seqs, slots, width = residual_in.shape
    rows = 256
    placed = pl.BlockSpec((None, rows, width), lambda s, c, meta: (meta[at], c, 0))
    fixed = lambda where, wide: pl.BlockSpec((None, rows, wide), lambda s, c, meta: (where, c, 0))
    extra = () if target is None else (target,)
    return order.call(
        finish_kernel,
        (grad_normed, residual_in, branch, gbc, weight, gain) + extra,
        meta=meta,
        grid=(1, slots // rows),
        in_specs=[
            fixed(0, width), placed, fixed(local, width), fixed(local, gbc.shape[2]),
            whole(weight.shape), whole(gain.shape),
        ] + [ANYWHERE] * len(extra),
        out_specs=[placed, whole((8, width))],
        out_shape=[SHAPE((seqs, slots, width), F32), SHAPE((8, width), F32)],
        aliases={7: 0} if extra else None,
        flops=1e9,
        moved=slots * width * 14,
        name="finish",
    )


def place(order, meta, own, got, at, seqs, target):
    count, slots, width = own.shape
    rows = 256
    plain = pl.BlockSpec((None, rows, width), lambda s, c, meta: (s, c, 0))
    placed = pl.BlockSpec((None, rows, width), lambda s, c, meta: (meta[at + s], c, 0))
    extra = () if target is None else (target,)
    return order.call(
        functools.partial(place_kernel, takes_at=2 * seqs),
        (own, got) + extra,
        meta=meta,
        grid=(count, slots // rows),
        in_specs=[plain, plain] + [ANYWHERE] * len(extra),
        out_specs=[placed],
        out_shape=[SHAPE((seqs, slots, width), own.dtype)],
        aliases={3: 0} if extra else None,
        flops=1e6,
        moved=count * slots * width * 6,
        name="place",
    )[0]


class Running:
    def __init__(self, order, steps):
        self.order, self.steps, self.value, self.ended = order, steps, None, False
        self.advance()

    def advance(self, times=1):
        for _ in range(times):
            if self.ended:
                return self
            try:
                self.sent = next(self.steps)
                self.order.before_next(*self.sent)
            except StopIteration as stop:
                self.value, self.ended = stop.value, True
        return self

    def pin(self):
        self.order.before_next(*(array[:8, :LANES].astype(F32) for array in self.sent))
        return self

    def end(self):
        while not self.ended:
            self.advance()
        return self.value


def line_sum(order, part, axis, finish, choose=True):
    count, mine = lax.axis_size(axis), lax.axis_index(axis)
    if count % 2:
        done = finish(lax.psum(part.astype(F32), axis))
        return done if choose else (done, done)
    middle = count // 2
    send = lambda value, pairs: lax.ppermute(value, axis, pairs)
    plus = lambda a, b: order.tie(a.astype(F32) + b.astype(F32))
    for k in range(middle - 1):
        pairs = [(k, k + 1), (count - 1 - k, count - 2 - k)]
        got = send(part, pairs)
        yield (part,)
        part = plus(part, got).astype(part.dtype)
    got = send(part, [(middle - 1, middle), (middle, middle - 1)])
    yield (part,)
    done = finish(plus(part, got))
    for k in range(middle - 1, 0, -1):
        got = send(done, [(k, k - 1), (count - 1 - k, count - k)])
        yield (done,)
        if k == 1 and not choose:
            return done, got
        takes = (mine == k - 1) | (mine == count - k)
        done = order.tie(jnp.where(takes, got, done))
    return done if choose else (done, done)


def crossed(order, value, axis, join):
    count = lax.axis_size(axis)
    pairs = lambda distance: [(i, (i + distance) % count) for i in range(count)]
    got = [lax.ppermute(value, axis, pairs(distance)) for distance in range(1, count)]
    yield (value,)
    for other in got:
        value = join(value, other)
    return order.tie(value)


def butterfly(order, value, axis, join):
    for bit in bits_of(axis):
        got = flipped(value, axis, bit)
        yield (value,)
        value = order.tie(join(value, got))
    return value


def bits_of(axis):
    size = lax.axis_size(axis)
    assert size & (size - 1) == 0
    return [1 << k for k in range(size.bit_length() - 1)]


def flipped(value, axis, bit):
    return lax.ppermute(value, axis, [(i, i ^ bit) for i in range(lax.axis_size(axis))])


def joined(one, two):
    state = lax.broadcasted_iota(I32, one.shape, 0) < STATE
    return jnp.where(state, two[STATE : STATE + 1] * one + two, one * two)


def carried(order, payload, axis, backward):
    mine, size = lax.axis_index(axis), lax.axis_size(axis)
    steps = bits_of(axis)
    odd = (mine & 1) == 1
    own = jnp.where(odd, payload[1], payload[0])
    give = jnp.where(odd, payload[0], payload[1])
    got = flipped(give, axis, 1)
    yield (give,)
    is_first = odd if backward else jnp.logical_not(odd)
    got = order.tie(got)
    one, two = jnp.where(is_first, own, got), jnp.where(is_first, got, own)
    total = joined(one, two)
    entering = jnp.broadcast_to((lax.iota(I32, total.shape[0]) >= STATE).astype(F32)[:, None], total.shape)
    for bit in steps[1:]:
        later = ((mine & bit) == 0) if backward else ((mine & bit) != 0)
        last = bit == steps[-1]
        pairs = [(i, i ^ bit) for i in range(size) if not last or bool(i & bit) == backward]
        got = lax.ppermute(total, axis, pairs)
        yield (total,)
        got = order.tie(got)
        entering = jnp.where(later, joined(got, entering), entering)
        if not last:
            total = joined(jnp.where(later, got, total), jnp.where(later, total, got))
    second = joined(entering, one)
    mine_now, other_now = jnp.where(is_first, entering, second), jnp.where(is_first, second, entering)
    back = flipped(other_now, axis, 1)
    yield (other_now,)
    return jnp.stack([jnp.where(odd, back, mine_now), jnp.where(odd, mine_now, back)])


def butterfly_sum(value, axis):
    for bit in bits_of(axis):
        value = value + flipped(value, axis, bit)
    return value


def gathered(value, axis):
    return lax.all_gather(value, axis, axis=1, tiled=True)


def shifted(block, axis, distance):
    devices = range(lax.axis_size(axis))
    route = [(i - distance, i) for i in devices if i - distance in devices]
    return lax.ppermute(block, axis, route)


BRANCH_SCALE = 64.0


def pad_lanes(value, width):
    return jnp.pad(value, [(0, 0)] * (value.ndim - 1) + [(0, width - value.shape[-1])])


def edge_terms(halo, taps):
    ext = jnp.concatenate([jnp.zeros_like(halo), halo], axis=1)
    return sum(taps[CONV - 1 - j] * ext[:, j : j + 8] for j in range(1, CONV))


def per_device(
    residual_in, lengths, norm_gain, gate_projection_weight, head_channels_weight, input_state_pair_weight,
    step_size_weight, x_taps, bc_taps, x_bias, bc_bias, step_bias, decay_log, skip_gain, out_gain,
    output_projection_weight, cotangent,
):
    seqs, slots, width = residual_in.shape
    channels = head_channels_weight.shape[1]
    own = input_state_pair_weight.shape[1]
    heads = step_size_weight.shape[1]
    head_at = lax.axis_index("head")
    count = seqs // GROUPS
    groups = range(GROUPS)
    dot = lambda spec, a, b: jnp.einsum(spec, a, b, preferred_element_type=F32)

    order = Order()
    run = lambda steps: Running(order, steps)

    meta, head, chan, expand = constants(lengths, step_bias, decay_log, skip_gain, out_gain, slots)

    before = shifted(residual_in[:, slots - 8 :], "seq", 1)
    pair_rows = gathered(
        jnp.concatenate(
            [input_state_pair_weight.astype(F32), bc_taps, bc_bias[None], jnp.zeros((3, own), F32)], axis=0
        ),
        "head",
    )
    pair_weight = pair_rows[:width].astype(BF16)
    bc_taps_all, bc_bias_all = pair_rows[width : width + CONV], pair_rows[width + CONV : width + CONV + 1]
    step_weight = pad_lanes(step_size_weight, LANES)
    bias = x_bias[None]
    gain_row = norm_gain[None]

    normed, branch_grad, proj, bc_raw, xs, bcs, sc, grad_hidden, cot_peak, inputs = ([None] * GROUPS for _ in range(10))
    starts, partials, mixed, states, final, ends = ([None] * GROUPS for _ in range(6))
    hidden, grad_gate, dy, grad_ins, gain_acc = ([None] * GROUPS for _ in range(5))
    branches, sums_of = {}, {}

    def project_of(g):
        normed[g], branch_grad[g], proj[g], grad_hidden[g], cot_peak[g], inputs[g] = project(
            order, meta, residual_in, cotangent, gain_row, gate_projection_weight, head_channels_weight, step_weight,
            output_projection_weight, g * count, count,
        )

    def states_of(g):
        xs[g], bc_raw[g], bcs[g], sc[g], ends[g] = local_states(
            order, meta, proj[g], normed[g], pair_weight, halo_x, halo_bc, x_taps, bias, bc_taps_all, bc_bias_all,
            head, g * count, channels,
        )
        starts[g] = run(carried(order, ends[g], "seq", False))

    def mix_of(g):
        mixed[g], sums, states[g], final[g] = mix(
            order, meta, xs[g], bcs[g], sc[g], starts[g].end(), proj[g], grad_hidden[g], chan
        )
        sums_of[g] = run(crossed(order, sums, "head", lambda a, b: a + b))

    def gate_of(g):
        hidden[g], grad_gate[g], dy[g], grad_end, gain_acc[g] = gate_back(
            order, meta, g * count, mixed[g], proj[g], grad_hidden[g], sums_of[g].end(), bcs[g], sc[g], chan
        )
        grad_ins[g] = run(carried(order, grad_end, "seq", True))

    def branch_of(s):
        g, i = divmod(s, count)
        branch = (dot("mq,qh->mh", hidden[g][i], output_projection_weight) * BRANCH_SCALE).astype(F16)
        done = lambda total: (inputs[g][i].astype(F32) + total * (1.0 / BRANCH_SCALE)).astype(BF16)
        branches[s] = run(line_sum(order, branch, "head", done, choose=False))

    def result_of(s, target):
        own_rows, got = branches[s].end()
        return place(order, meta, own_rows[None], got[None], s, seqs, target)

    backs, gps, accs, haccs = [[] for _ in range(GROUPS)], {}, {}, {}
    parts, gbcs, baccs, gain_accs = {}, {}, [], []
    dbc_sums, fixes = {}, {}

    def scale_of():
        largest = jnp.max(functools.reduce(jnp.maximum, cot_peak))
        return run(butterfly(order, jnp.full((8, LANES), largest, F32), "seq", jnp.maximum))

    def back_of(s):
        g, i = divmod(s, count)
        *backs[g], accs[s], haccs[s] = state_back(
            order, meta, i, g * count, proj[g], halo_x, bcs[g], sc[g], dy[g], mixed[g], states[g], final[g],
            grad_ins[g].end(), grad_gate[g], x_taps, bias, head, chan, expand, backs[g] or None,
        )

    def edges_of(g):
        gps[g], _, tail, edge = backs[g]
        fixes[g] = (shifted(edge, "seq", -1), tail[:, -1])
        order.before_next(edge)

    def pair_sum_of(g):
        dbc_sums[g] = run(line_sum(order, order.tie(backs[g][1]), "head", lambda total: total))

    def fix_of(g):
        got, tail = fixes[g]
        fixed = order.tie(tail + edge_terms(got, x_taps)).astype(BF16)
        gps[g] = lax.dynamic_update_slice(gps[g], fixed, (0, slots - 8, channels))

    def part_of(s):
        part = (dot("gl,ol->go", gps[s // count][s % count], weight) * scale[0]).astype(F16)
        parts[s] = run(line_sum(order, part, "head", lambda total: total.astype(F16)))

    def pair_of(g):
        gbc, btail, bedge, bacc = pair_back(
            order, meta, g * count, bc_raw[g], halo_bc, dbc_sums[g].end(), bc_taps_all, bc_bias_all
        )
        baccs.append(bacc)
        gbcs[g] = (gbc, btail, shifted(bedge, "seq", -1))
        order.before_next(bedge)

    def pair_fix(g):
        gbc, btail, got = gbcs[g]
        fixed = order.tie(btail + edge_terms(got, bc_taps_all)).astype(BF16)
        gbcs[g] = lax.dynamic_update_slice(gbc, fixed, (0, slots - 8, 0))

    def finish_of(s, target):
        g, i = divmod(s, count)
        total = parts[s].end().astype(F32) * scale[1]
        target, gain = finish(
            order, meta, total[None], residual_in, branch_grad[g], gbcs[g], pair_weight, gain_row, s, i, target
        )
        gain_accs.append(gain)
        return target

    add = lambda terms: functools.reduce(lambda a, b: a + b, terms)
    tied_dots = lambda spec, pairs: order.tie(add([dot(spec, a, b) for a, b in pairs]))
    project_of(0)
    project_of(1)
    halo_x, halo_bc = edge_halos(order, meta, before, gain_row, head_channels_weight, pair_weight)
    states_of(0)
    peak = scale_of()
    order.fence()
    weight = jnp.concatenate([gate_projection_weight, head_channels_weight, order.tie(step_weight)], axis=1)
    order.before_next(weight)
    starts[0].advance()
    states_of(1)
    peak.advance()
    starts[0].advance()
    order.fence()
    starts[1].advance()
    order.fence()
    starts[0].advance()
    starts[1].advance()
    peak.advance()
    mix_of(0)
    starts[1].advance()
    peak = jnp.maximum(peak.end()[0, 0], 1e-30)
    scale = 0.0625 / peak, 16.0 * peak
    mix_of(1)
    gate_of(0)
    branch_of(0)
    order.fence()
    grad_ins[0].advance()
    gate_of(1)
    grad_ins[0].advance()
    order.fence()
    branch_of(1)
    grad_ins[1].advance()
    order.fence()
    out_grad = tied_dots("yfx,yfw->xw", [(hidden[g], branch_grad[g]) for g in groups])
    order.before_next(out_grad)
    order.fence()
    grad_ins[0].advance()
    grad_ins[1].advance()
    branches[0].advance().pin()
    branch_of(2)
    back_of(0)
    branches[1].advance().pin()
    gate_grad = tied_dots("wji,wjr->ir", [(normed[g], grad_gate[g]) for g in groups])
    order.before_next(gate_grad)
    order.fence()
    grad_ins[1].advance()
    branch_of(3)
    branches[3].pin()
    back_of(1)
    early = lax.psum((out_grad, gate_grad), "seq")
    edges_of(0)
    branches[0].advance()
    branches[2].advance().pin()
    order.fence()
    fix_of(0)
    part_of(0)
    parts[0].pin()
    back_of(2)
    branches[1].advance()
    branches[3].advance().pin()
    result = result_of(0, None)
    pair_sum_of(0)
    back_of(3)
    edges_of(1)
    part_of(1)
    parts[1].pin()
    order.fence()
    parts[0].advance().pin()
    branches[2].advance()
    fix_of(1)
    dbc_sums[0].advance()
    result = result_of(1, result)
    pair_sum_of(1)
    part_of(2)
    parts[2].pin()
    order.fence()
    branches[3].advance()
    result = result_of(2, result)
    order.fence()
    parts[1].advance().pin()
    dbc_sums[0].advance()
    grad_x_weight = tied_dots("wji,wjr->ir", [(normed[g], gps[g][..., channels : 2 * channels]) for g in groups])
    grad_step_weight = tied_dots("wji,wjr->ir", [(normed[g], gps[g][..., 2 * channels :]) for g in groups])
    order.before_next(grad_x_weight, grad_step_weight)
    order.fence()
    dbc_sums[1].advance()
    part_of(3)
    parts[3].pin()
    parts[0].advance()
    result = result_of(3, result)
    zero = jnp.clip(early[0][0, 0] + early[1][0, 0], -1.0, 1.0) * 0.0
    late = lax.psum((grad_x_weight, grad_step_weight + zero), "seq")
    order.fence()
    parts[2].advance().pin()
    order.fence()
    parts[3].advance().pin()
    parts[1].advance().pin()
    order.fence()
    dbc_sums[1].advance()
    pair_of(0)
    pair_fix(0)
    grad_input = finish_of(0, None)
    parts[2].advance().pin()
    out_result, gate_result = order.tie(early[0]), order.tie(early[1])
    order.before_next(out_result, gate_result)
    order.fence()
    grad_input = finish_of(1, grad_input)
    parts[3].advance().pin()
    order.fence()
    pair_of(1)
    pair_fix(1)
    grad_pair = add(dot("wji,wjr->ir", normed[g], gbcs[g]) for g in groups)
    grad_own = lax.dynamic_slice(grad_pair, (0, head_at * own), (width, own))
    x_result, step_result = order.tie(late[0]), order.tie(late[1])
    order.before_next(x_result)
    order.fence()
    grad_input = finish_of(2, grad_input)
    grad_input = finish_of(3, grad_input)
    acc = jnp.sum(add(accs.values()).reshape(6, 8, channels), axis=1)
    acc = jnp.concatenate([acc, jnp.sum(add(gain_acc), axis=0)[None]], axis=0)
    hacc = jnp.sum(add(haccs.values()).reshape(2, 8, LANES), axis=1)
    bacc = jnp.sum(add(baccs).reshape(5, 8, 2 * STATE), axis=1)
    flat = jnp.concatenate([acc.reshape(-1), hacc.reshape(-1), bacc.reshape(-1), grad_own.reshape(-1)])
    flat = butterfly_sum(flat.reshape(-1, LANES), "seq").reshape(-1)
    ends_at = [acc.size, acc.size + hacc.size, acc.size + hacc.size + bacc.size]
    acc, hacc, bacc, grad_own = (
        piece.reshape(like.shape) for piece, like in zip(jnp.split(flat, ends_at), (acc, hacc, bacc, grad_own))
    )
    bacc = lax.dynamic_slice(bacc, (0, head_at * own), (5, own))
    gain = butterfly_sum(jnp.sum(add(gain_accs), axis=0).reshape(-1, LANES), "seq").reshape(-1)
    return (
        result,
        grad_input,
        gain,
        gate_result,
        x_result,
        grad_own,
        step_result[:, :heads],
        acc[:CONV],
        bacc[:CONV],
        acc[CONV],
        bacc[CONV],
        hacc[0, :heads],
        hacc[1, :heads],
        jnp.sum(acc[5].reshape(heads, HEAD_DIM), axis=1),
        acc[6],
        out_result,
    )


def solution(mesh):
    return jax.shard_map(
        per_device,
        mesh=mesh,
        in_specs=(
            P(None, "seq", None), P(), P(), P(None, "head"), P(None, "head"), P(None, "head"), P(None, "head"),
            P(None, "head"), P(None, "head"), P("head"), P("head"), P("head"), P("head"), P("head"), P("head"),
            P("head", None), P(None, "seq", None),
        ),
        out_specs=(
            P(None, "seq", None), P(None, "seq", None), P(), P(None, "head"), P(None, "head"), P(None, "head"),
            P(None, "head"), P(None, "head"), P(None, "head"), P("head"), P("head"), P("head"), P("head"),
            P("head"), P("head"), P("head", None),
        ),
        check_vma=False,
    )
```
